32 devices in a mesh: tm: 8 (over y, x, core), user: 4 (over z).
Axes of the slice: x: 2, y: 2, z: 4, core: 2. Of those that a mesh axis runs over, the one named last changes fastest.
Arguments:
- events: bfloat16 [4, 8192, 512], P('user', 'tm'), may hold values from -6 to 6
- w_first: bfloat16 [512, 1024], replicated, may hold values from -0.25 to 0.25
- b_first: float32 [1024], replicated, may hold values from -3 to 3
- w_second: bfloat16 [1024, 512], replicated, may hold values from -0.1875 to 0.1875
- count_embed: float32 [512], replicated, may hold values from -0.3 to 0.3
- norm_gain: float32 [512], replicated, may hold values from 0.5 to 1.5
- event_session: int32 [4, 8192], P('user', 'tm'), may hold values from 0 to 511, as said below
- event_count: int32 [4, 8], P('user', 'tm'), may hold values from 256 to 1024, as said below
- session_user: int32 [4, 512], P('user', 'tm'), may hold values from 0 to 65535, as said below
Outputs:
- section_rows: bfloat16 [8, 4, 128, 512], P('tm', 'user')
- section_users: int32 [8, 4, 128], P('tm', 'user')
The draws below stay inside these ranges and needn't reach their ends.
Inputs may be any that keep to these rules, and one draw needn't show every extreme that they name: `event_session`: the events of time slice t (slots t * 1024 to (t + 1) * 1024 - 1 of a shard) name sessions of slices max(0, t - 4) to t only; some sessions have no valid event. `event_count`: some time slice of some shard has all 1024 events valid. `session_user`: among the 64 sessions of one shard and time slice, at most 32 have users of the same section (user mod 4); in every time slice some section gets exactly 32 from every shard.
All inputs are finite; a program needn't handle non-finite values.
Results may differ from the reference program's by a relative error of at most 0.0042.
Values may be sent and summed in bfloat16 or wider, within the bound.
A program may use at most 64 MiB of HBM per device.

```python
import jax
import jax.numpy as jnp
from jax import lax

D = 512
FF = 1024
EV_DEV = 1024
SESS_DEV = 64
USERS = 65536
SECTIONS = 4
SESS_G = 512
EVENTS_G = 8192
CAP = 32
N_TM = 8
N_USER = 4


def draw_event_count(key, part):
    slices = SESS_G // SESS_DEV
    key_count, key_fullest = jax.random.split(jax.random.fold_in(key, 11))
    counts = jax.random.randint(key_count, (SECTIONS * slices,), EV_DEV // 4, EV_DEV + 1)
    fullest = jax.random.randint(key_fullest, (), 0, SECTIONS * slices)
    flattened = jnp.where(jnp.arange(SECTIONS * slices) == fullest, EV_DEV, counts)
    return flattened.reshape(SECTIONS, slices).astype(jnp.int32)


def draw_event_session(key, part):
    slices = SESS_G // SESS_DEV
    half_reach = slices // 2
    key_dead, key_offset = jax.random.split(jax.random.fold_in(key, 23))
    alive_table = jax.random.randint(key_dead, (SECTIONS, SESS_G), 0, 6) != 0
    slice_of = jnp.arange(slices * EV_DEV, dtype=jnp.int32) // EV_DEV
    first_slice = jnp.maximum(slice_of - half_reach, 0)
    span = (slice_of - first_slice + 1) * SESS_DEV
    offsets = jax.random.randint(key_offset, (4, SECTIONS, slices * EV_DEV), 0, 2 ** 30) % span
    candidate = first_slice * SESS_DEV + offsets
    chosen = candidate[3]
    for attempt in (2, 1, 0):
        living = jnp.take_along_axis(alive_table, candidate[attempt], axis=1)
        chosen = jnp.where(living, candidate[attempt], chosen)
    return chosen.astype(jnp.int32)


def draw_session_user(key, part):
    slices = SESS_G // SESS_DEV
    width = SECTIONS * CAP
    slots = jnp.arange(width)
    block_keys = jax.random.split(jax.random.fold_in(key, 41), SECTIONS * slices)
    first_slice = jax.random.randint(jax.random.fold_in(key, 43), (slices,), 0, SECTIONS)
    first_column = jnp.tile(first_slice, SECTIONS)

    def arrange(block_key, column_full):
        key_slot, key_place, key_member = jax.random.split(block_key, 3)
        scores = jax.random.randint(key_slot, (width,), 0, 2 ** 20) * width + slots
        scores = jnp.where(slots // CAP == column_full, slots - width, scores)
        order = jnp.argsort(scores)
        columns = order[:SESS_DEV] // CAP
        placing = jax.random.randint(key_place, (SESS_DEV,), 0, 2 ** 20) * SESS_DEV + jnp.arange(SESS_DEV)
        columns = columns[jnp.argsort(placing)]
        member = jax.random.randint(key_member, (SESS_DEV,), 0, USERS // SECTIONS)
        return columns + SECTIONS * member
    result = jax.vmap(arrange)(block_keys, first_column)
    return result.reshape(SECTIONS, slices * SESS_DEV).astype(jnp.int32)


def steps_of(stream_key, extent, cuts, least, high):
    loudness = 1.0
    for position, blocks in cuts:
        draws = jax.random.uniform(jax.random.fold_in(jax.random.fold_in(stream_key, 6), position), (blocks,), jnp.float32, least / len(cuts), high / len(cuts))
        loudness = loudness * jnp.repeat(jnp.exp(draws), extent[position] // blocks).reshape((-1,) + (1,) * (len(extent) - 1 - position))
    return loudness


def gaussian(stream_key, shape, spread, reach, pieces=(), held_as=jnp.bfloat16):
    entries = spread * jax.random.normal(stream_key, shape, jnp.float32)
    if pieces:
        entries = entries * steps_of(stream_key, shape, pieces, -0.22, 0.18)
    return jnp.clip(entries, -reach, reach).astype(held_as)


def setup_inputs(seed: int = 0) -> dict:
    splits = jax.random.split(jax.random.key(seed), 10)
    return {
        "events": gaussian(splits[0], (N_USER, EVENTS_G, D), 1.0, 6.0, ((0, 4), (1, 8))),
        "w_first": gaussian(splits[1], (D, FF), D ** -0.5, 0.25),
        "b_first": gaussian(splits[2], (FF,), 0.5, 3.0, (), jnp.float32),
        "w_second": gaussian(splits[3], (FF, D), FF ** -0.5, 0.1875),
        "count_embed": gaussian(splits[4], (D,), 0.05, 0.3, (), jnp.float32),
        "norm_gain": jnp.clip(1.0 + 0.1 * jax.random.normal(splits[5], (D,), jnp.float32), 0.5, 1.5),
        "event_session": draw_event_session(jax.random.fold_in(splits[9], 71), 0),
        "event_count": draw_event_count(jax.random.fold_in(splits[9], 71), 0),
        "session_user": draw_session_user(jax.random.fold_in(splits[9], 71), 0),
    }


def embed(event_rows, w_first, b_first, w_second):
    hidden = jax.nn.gelu(jnp.dot(event_rows, w_first, preferred_element_type=jnp.float32) + b_first).astype(jnp.bfloat16)
    return jnp.dot(hidden, w_second, preferred_element_type=jnp.float32).astype(jnp.bfloat16)

def reference(events, w_first, b_first, w_second, count_embed, norm_gain, event_session, event_count, session_user):

    def shard_sums(packed):
        event_rows, session_ids, slice_counts = packed
        vectors = embed(event_rows, w_first, b_first, w_second).astype(jnp.float32)
        within = jnp.arange(N_TM * EV_DEV) % EV_DEV
        valid = within < jnp.repeat(slice_counts, EV_DEV)
        target = jnp.where(valid, session_ids, SESS_G)
        sums = jax.ops.segment_sum(vectors, target, SESS_G + 1)[:SESS_G]
        totals = jax.ops.segment_sum(valid.astype(jnp.float32), target, SESS_G + 1)[:SESS_G]
        return (sums, totals)
    sums, totals = lax.map(shard_sums, (events, event_session, event_count))
    averaged = sums / jnp.maximum(totals, 1.0)[..., None]
    mixed = averaged + jnp.log1p(totals)[..., None] * count_embed
    scaled = mixed * lax.rsqrt(lax.optimization_barrier(jnp.mean(mixed * mixed, axis=-1, keepdims=True)) + 1e-06) * norm_gain
    session_rows = scaled.astype(jnp.bfloat16).reshape(N_USER, N_TM, SESS_DEV, D)
    users = session_user.reshape(N_USER, N_TM, SESS_DEV)
    section = users % N_USER
    same = section[..., :, None] == section[..., None, :]
    before = jnp.arange(SESS_DEV)[:, None] > jnp.arange(SESS_DEV)[None, :]
    rank = lax.optimization_barrier(jnp.sum((same & before).astype(jnp.int32), axis=-1))
    slot = section * CAP + rank
    assign = slot[..., None, :] == jnp.arange(N_USER * CAP)[:, None]
    placed = jnp.einsum('utcs,utsd->tucd', assign.astype(jnp.float32), session_rows.astype(jnp.float32))
    placed = placed.reshape(N_TM, N_USER, N_USER, CAP, D).transpose(0, 2, 1, 3, 4)
    section_rows = placed.reshape(N_TM, N_USER, N_USER * CAP, D).astype(jnp.bfloat16)
    slot_users = lax.optimization_barrier(jnp.sum(jnp.where(assign, users[..., None, :] + 1, 0), axis=-1)) - 1
    slot_users = slot_users.reshape(N_USER, N_TM, N_USER, CAP).transpose(1, 2, 0, 3)
    section_users = slot_users.reshape(N_TM, N_USER, N_USER * CAP).astype(jnp.int32)
    return (section_rows, section_users)
```

```python
import functools
import math

import jax
import jax.numpy as jnp
from jax import lax
from jax.experimental import pallas as pl
from jax.experimental.pallas import tpu as pltpu
from jax.sharding import PartitionSpec as P

MESH = pl.DeviceIdType.MESH
BF16 = jnp.bfloat16
F32 = jnp.float32
I32 = jnp.int32


def iota(shape, axis):
    return lax.broadcasted_iota(I32, shape, axis)


def kernel(
    n_tm,
    n_sec,
    reach,
    cap,
    events,
    w_first,
    w_second,
    b_first,
    count_embed,
    norm_gain,
    event_session,
    event_count,
    session_user,
    out_rows,
    out_users,
    ev_v,
    w1_v,
    w2_v,
    acc,
    cnt,
    sums_send,
    sums_recv,
    cnt_recv,
    rows_send,
    rows_recv,
    users_send,
    users_recv,
    load_sem,
    sums_ss,
    sums_rs,
    cnt_ss,
    cnt_rs,
    rows_ss,
    rows_rs,
    users_ss,
    users_rs,
):
    t = lax.axis_index("tm")
    u = lax.axis_index("user")
    ev_rows, width = ev_v.shape
    hidden = w1_v.shape[1]
    sess = session_user.shape[1]
    held = (reach + 1) * sess
    step = min(256, hidden)

    loads = []
    pairs = ((w_first, w1_v), (events.at[0], ev_v), (w_second, w2_v))
    for i, (src, dst) in enumerate(pairs):
        load = pltpu.make_async_copy(src, dst, load_sem.at[i])
        load.start()
        loads.append(load)

    barrier = pltpu.get_barrier_semaphore()
    for d in range(1, reach + 1):

        @pl.when(t + d < n_tm)
        def _(d=d):
            pl.semaphore_signal(
                barrier, inc=1, device_id={"tm": t + d}, device_id_type=MESH
            )

    for k in range(1, n_sec):
        pl.semaphore_signal(
            barrier,
            inc=1,
            device_id={"user": lax.rem(u + k, n_sec)},
            device_id_type=MESH,
        )

    def sums_copy(d):
        return pltpu.make_async_remote_copy(
            src_ref=sums_send.at[d - 1],
            dst_ref=sums_recv.at[d - 1],
            send_sem=sums_ss.at[d - 1],
            recv_sem=sums_rs.at[d - 1],
            device_id={"tm": t - d},
            device_id_type=MESH,
        )

    def cnt_copy(d):
        return pltpu.make_async_remote_copy(
            src_ref=cnt.at[d],
            dst_ref=cnt_recv.at[d - 1],
            send_sem=cnt_ss.at[d - 1],
            recv_sem=cnt_rs.at[d - 1],
            device_id={"tm": t - d},
            device_id_type=MESH,
        )

    def routed_copy(k, send, recv, ss, rs):
        v = lax.rem(u + k, n_sec)
        return pltpu.make_async_remote_copy(
            src_ref=send.at[v],
            dst_ref=recv.at[u],
            send_sem=ss.at[k - 1],
            recv_sem=rs.at[k - 1],
            device_id={"user": v},
            device_id_type=MESH,
        )

    def rows_copy(k):
        return routed_copy(k, rows_send, rows_recv, rows_ss, rows_rs)

    def users_copy(k):
        return routed_copy(k, users_send, users_recv, users_ss, users_rs)

    ids = event_session[...]
    block = t - ids // sess
    local = block * sess + lax.rem(ids, sess)
    lane = iota((1, ev_rows), 1)
    local = jnp.where(lane < event_count[...], local, -1)
    belongs = jnp.where(local == iota((held, ev_rows), 0), 1.0, 0.0)
    assign = belongs.astype(BF16)
    totals = jnp.sum(belongs, axis=1, keepdims=True)
    cnt[...] = jnp.broadcast_to(totals, (held, 128)).reshape(reach + 1, sess, 128)

    user_row = session_user[...]
    square = iota((sess, sess), 0), iota((sess, sess), 1)
    user_col = jnp.sum(
        jnp.where(square[0] == square[1], user_row, 0), axis=1, keepdims=True
    )
    sec_row = lax.rem(user_row, n_sec)
    sec_col = lax.rem(user_col, n_sec)
    same = jnp.where(sec_row == sec_col, 1, 0)
    rank_row = jnp.sum(
        jnp.where(square[0] < square[1], same, 0), axis=0, keepdims=True
    )
    rank_col = jnp.sum(
        jnp.where(square[1] < square[0], same, 0), axis=1, keepdims=True
    )
    padded = rows_send.shape[1]
    place = jnp.where(
        sec_row * padded + rank_row == iota((n_sec * padded, sess), 0), 1.0, 0.0
    ).astype(BF16)
    slots = n_sec * cap
    at = iota((sess, slots), 1) == rank_col + u * cap
    for v in range(n_sec):
        named = jnp.where(at & (sec_col == v), user_col + 1, 0)
        users_send[v] = jnp.broadcast_to(
            jnp.sum(named, axis=0, keepdims=True), (8, slots)
        )

    c_one = math.sqrt(2.0 / math.pi)
    c_three = c_one * 0.044715

    def part(i):
        cols = slice(i * step, (i + 1) * step)
        x = jnp.dot(ev_v[...], w1_v[:, cols], preferred_element_type=F32)
        x = x + b_first[:, cols]
        twice = x + x * jnp.tanh(x * (c_one + c_three * (x * x)))
        pooled = jnp.dot(assign, twice.astype(BF16), preferred_element_type=F32)
        return jnp.dot(pooled.astype(BF16), w2_v[cols, :], preferred_element_type=F32)

    loads[0].wait()
    loads[1].wait()
    loads[2].wait()
    acc[...] = part(0)

    pl.semaphore_wait(barrier, jnp.minimum(t, reach) + n_sec - 1)
    for k in range(1, n_sec):
        users_copy(k).start()
    for d in range(reach, 0, -1):

        @pl.when(t >= d)
        def _(d=d):
            cnt_copy(d).start()

    for i in range(1, hidden // step):
        acc[...] += part(i)

    for d in range(reach, 0, -1):

        @pl.when(t >= d)
        def _(d=d):
            sums_send[d - 1] = acc[d * sess : (d + 1) * sess].astype(BF16)
            sums_copy(d).start()

    for d in range(1, reach + 1):

        @pl.when(t + d < n_tm)
        def _(d=d):
            cnt_copy(d).wait_recv()
            sums_copy(d).wait_recv()
            acc[:sess] += sums_recv[d - 1].astype(F32)
            cnt[0] += cnt_recv[d - 1]

    count = cnt[0][:, :1]
    mixed = acc[:sess] * (0.5 / jnp.maximum(count, 1.0))
    mixed = mixed + jnp.log(1.0 + count) * count_embed[...]
    mean = jnp.mean(mixed * mixed, axis=1, keepdims=True)
    rows = (mixed * lax.rsqrt(mean + 1e-06) * norm_gain[...]).astype(BF16)
    outgoing = jnp.dot(place, rows, preferred_element_type=F32).astype(BF16)
    rows_send[...] = outgoing.reshape(n_sec, padded, width)
    for k in range(1, n_sec):
        rows_copy(k).start()
    rows_recv[u] = rows_send[u]
    users_recv[u] = users_send[u]

    for k in range(1, n_sec):
        users_copy(k).wait_recv()
    out_users[0] = jnp.sum(users_recv[...], axis=0)[:1] - 1
    for k in range(1, n_sec):
        rows_copy(k).wait_recv()
    if padded == cap:
        out_rows[0, 0] = rows_recv[...].reshape(slots, width)
    else:
        kept = rows_recv[...].astype(F32)[:, :cap]
        out_rows[0, 0] = kept.reshape(slots, width).astype(BF16)

    for d in range(1, reach + 1):

        @pl.when(t >= d)
        def _(d=d):
            cnt_copy(d).wait_send()
            sums_copy(d).wait_send()

    for k in range(1, n_sec):
        users_copy(k).wait_send()
        rows_copy(k).wait_send()


def on_device(
    n_tm,
    n_sec,
    events,
    w_first,
    b_first,
    w_second,
    count_embed,
    norm_gain,
    event_session,
    event_count,
    session_user,
):
    _, ev_rows, width = events.shape
    hidden = w_first.shape[1]
    sess = session_user.shape[1]
    reach = n_tm // 2
    cap = max(2, 2 * sess // n_sec)
    padded = -(-cap // 16) * 16
    slots = n_sec * cap
    held = (reach + 1) * sess
    dma = pltpu.SemaphoreType.DMA
    vmem = pl.BlockSpec(memory_space=pltpu.VMEM)
    hbm = pl.BlockSpec(memory_space=pl.ANY)
    return pl.pallas_call(
        functools.partial(kernel, n_tm, n_sec, reach, cap),
        out_shape=(
            jax.ShapeDtypeStruct((1, 1, slots, width), BF16),
            jax.ShapeDtypeStruct((1, 1, slots), I32),
        ),
        in_specs=[hbm] * 3 + [vmem] * 6,
        out_specs=(vmem, vmem),
        scratch_shapes=[
            pltpu.VMEM((ev_rows, width), BF16),
            pltpu.VMEM((width, hidden), BF16),
            pltpu.VMEM((hidden, width), BF16),
            pltpu.VMEM((held, width), F32),
            pltpu.VMEM((reach + 1, sess, 128), F32),
            pltpu.VMEM((reach, sess, width), BF16),
            pltpu.VMEM((reach, sess, width), BF16),
            pltpu.VMEM((reach, sess, 128), F32),
            pltpu.VMEM((n_sec, padded, width), BF16),
            pltpu.VMEM((n_sec, padded, width), BF16),
            pltpu.VMEM((n_sec, 8, slots), I32),
            pltpu.VMEM((n_sec, 8, slots), I32),
            dma((3,)),
            dma((reach,)),
            dma((reach,)),
            dma((reach,)),
            dma((reach,)),
            dma((n_sec - 1,)),
            dma((n_sec - 1,)),
            dma((n_sec - 1,)),
            dma((n_sec - 1,)),
        ],
        compiler_params=pltpu.CompilerParams(
            collective_id=0, has_side_effects=True, vmem_limit_bytes=48 << 20
        ),
        name="pool_and_route",
    )(
        events,
        w_first,
        w_second,
        b_first.reshape(1, hidden),
        count_embed.reshape(1, width),
        norm_gain.reshape(1, width),
        event_session,
        event_count,
        session_user,
    )


def solution(mesh):
    in_specs = (
        P("user", "tm", None),
        P(),
        P(),
        P(),
        P(),
        P(),
        P("user", "tm"),
        P("user", "tm"),
        P("user", "tm"),
    )
    out_specs = (P("tm", "user", None, None), P("tm", "user", None))
    return jax.shard_map(
        functools.partial(on_device, mesh.shape["tm"], mesh.shape["user"]),
        mesh=mesh,
        in_specs=in_specs,
        out_specs=out_specs,
        check_vma=False,
    )
```

```python
import functools
import math

import jax
import jax.numpy as jnp
from jax import lax
from jax.experimental import pallas as pl
from jax.experimental.pallas import tpu as pltpu
from jax.sharding import PartitionSpec as P

MESH = pl.DeviceIdType.MESH
BF16 = jnp.bfloat16
F32 = jnp.float32
I32 = jnp.int32
VMEM_BYTES = 63 << 20


def iota(shape, axis):
    return lax.broadcasted_iota(I32, shape, axis)


def kernel(
    n_tm,
    n_sec,
    reach,
    cap,
    events,
    w_first,
    w_second,
    b_first,
    count_embed,
    norm_gain,
    event_session,
    event_count,
    session_user,
    out_rows,
    out_users,
    ev_v,
    w1_v,
    w2_v,
    b1_v,
    embed_v,
    gain_v,
    ids_v,
    count_v,
    user_v,
    acc,
    cnt_send,
    cnt_recv,
    pair_send,
    pair_recv,
    sums_send,
    sums_recv,
    rows_send,
    rows_recv,
    users_send,
    users_recv,
    small_sem,
    ev_sem,
    w1_sem,
    w2_sem,
    pair_sem,
    sums_ss,
    sums_rs,
    cnt_ss,
    cnt_rs,
    rows_ss,
    rows_rs,
    users_ss,
    users_rs,
):
    t = lax.axis_index("tm")
    u = lax.axis_index("user")
    odd = lax.rem(t, 2)
    partner = t + 1 - 2 * odd
    ev_rows, width = ev_v.shape
    hidden = w1_v.shape[1]
    sess = user_v.shape[1]
    held = (reach + 1) * sess
    half = reach // 2
    crossing = half * sess
    step = min(256, hidden)
    parts = hidden // step

    def load(src, dst, sem):
        copy = pltpu.make_async_copy(src, dst, sem)
        copy.start()
        return copy

    small = [
        load(src, dst, small_sem.at[i])
        for i, (src, dst) in enumerate(
            (
                (event_session, ids_v),
                (event_count, count_v),
                (session_user, user_v),
                (b_first, b1_v),
                (count_embed, embed_v),
                (norm_gain, gain_v),
            )
        )
    ]
    w1_load, w2_load = [], []
    for i in range(parts):
        cols = pl.ds(i * step, step)
        w1_load.append(load(w_first.at[:, cols], w1_v.at[:, cols], w1_sem.at[i]))
        if i == 0:
            ev_load = load(events.at[0], ev_v, ev_sem)
    for i in range(parts):
        cols = pl.ds(i * step, step)
        w2_load.append(load(w_second.at[cols], w2_v.at[cols], w2_sem.at[i]))

    barrier = pltpu.get_barrier_semaphore()

    def greet(device):
        pl.semaphore_signal(barrier, inc=1, device_id=device, device_id_type=MESH)

    for d in range(1, reach + 1):

        @pl.when(t + d < n_tm)
        def _(d=d):
            greet({"tm": t + d})

    @pl.when(odd == 1)
    def _():
        greet({"tm": t - 1})

    for k in range(1, n_sec):
        greet({"user": lax.rem(u + k, n_sec)})

    def pair_copy():
        return pltpu.make_async_remote_copy(
            src_ref=pair_send,
            dst_ref=pair_recv,
            send_sem=pair_sem.at[0],
            recv_sem=pair_sem.at[1],
            device_id={"tm": partner},
            device_id_type=MESH,
        )

    def sums_copy(j):
        return pltpu.make_async_remote_copy(
            src_ref=sums_send.at[j - 1],
            dst_ref=sums_recv.at[j - 1],
            send_sem=sums_ss.at[j - 1],
            recv_sem=sums_rs.at[j - 1],
            device_id={"tm": t - 2 * j},
            device_id_type=MESH,
        )

    def cnt_copy(d):
        return pltpu.make_async_remote_copy(
            src_ref=cnt_send.at[d],
            dst_ref=cnt_recv.at[d - 1],
            send_sem=cnt_ss.at[d - 1],
            recv_sem=cnt_rs.at[d - 1],
            device_id={"tm": t - d},
            device_id_type=MESH,
        )

    def routed_copy(k, send, recv, ss, rs):
        v = lax.rem(u + k, n_sec)
        return pltpu.make_async_remote_copy(
            src_ref=send.at[v],
            dst_ref=recv.at[u],
            send_sem=ss.at[k - 1],
            recv_sem=rs.at[k - 1],
            device_id={"user": v},
            device_id_type=MESH,
        )

    def rows_copy(k):
        return routed_copy(k, rows_send, rows_recv, rows_ss, rows_rs)

    def users_copy(k):
        return routed_copy(k, users_send, users_recv, users_ss, users_rs)

    for copy in small:
        copy.wait()
    ids = ids_v[...]
    d_of = t - ids // sess
    block = d_of // 2 + jnp.where(lax.rem(d_of, 2) == 0, half, 0)
    local = block * sess + lax.rem(ids, sess)
    lane = iota((1, ev_rows), 1)
    local = jnp.where(lane < count_v[...], local, -1)
    belongs = jnp.where(local == iota((held, ev_rows), 0), 1.0, 0.0)
    assign = belongs.astype(BF16)
    totals = jnp.sum(belongs, axis=1, keepdims=True)
    diagonal = iota((sess, 128), 0) == iota((sess, 128), 1)
    for d in range(reach + 1):
        first = (d // 2 + (half if d % 2 == 0 else 0)) * sess
        as_row = jnp.where(diagonal, totals[first : first + sess], 0.0)
        cnt_send[d] = jnp.broadcast_to(
            jnp.sum(as_row, axis=0, keepdims=True), (8, 128)
        )

    user_row = user_v[...]
    square = iota((sess, sess), 0), iota((sess, sess), 1)
    user_col = jnp.sum(
        jnp.where(square[0] == square[1], user_row, 0), axis=1, keepdims=True
    )
    sec_row = lax.rem(user_row, n_sec)
    sec_col = lax.rem(user_col, n_sec)
    same = jnp.where(sec_row == sec_col, 1, 0)
    rank_row = jnp.sum(
        jnp.where(square[0] < square[1], same, 0), axis=0, keepdims=True
    )
    rank_col = jnp.sum(
        jnp.where(square[1] < square[0], same, 0), axis=1, keepdims=True
    )
    padded = rows_send.shape[1]
    place = jnp.where(
        sec_row * padded + rank_row == iota((n_sec * padded, sess), 0), 1.0, 0.0
    ).astype(BF16)
    slots = n_sec * cap
    at = iota((sess, slots), 1) == rank_col + u * cap
    for v in range(n_sec):
        named = jnp.where(at & (sec_col == v), user_col + 1, 0)
        users_send[v] = jnp.broadcast_to(
            jnp.sum(named, axis=0, keepdims=True), (8, slots)
        )

    c_one = math.sqrt(2.0 / math.pi)
    c_three = c_one * 0.044715

    def first_product(i):
        w1_load[i].wait()
        cols = slice(i * step, (i + 1) * step)
        x = jnp.dot(ev_v[...], w1_v[:, cols], preferred_element_type=F32)
        return x + b1_v[:, cols]

    def activate(x):
        twice = x + x * jnp.tanh(x * (c_one + c_three * (x * x)))
        return twice.astype(BF16)

    def second_product(i, active, rows):
        cols = slice(i * step, (i + 1) * step)
        pooled = jnp.dot(assign[rows], active, preferred_element_type=F32)
        return jnp.dot(pooled.astype(BF16), w2_v[cols, :], preferred_element_type=F32)

    ev_load.wait()
    x = first_product(0)
    for i in range(parts):
        following = first_product(i + 1) if i + 1 < parts else None
        active = activate(x)
        w2_load[i].wait()
        if i + 1 < parts:
            term = second_product(i, active, slice(0, held))
            acc[...] = term if i == 0 else acc[...] + term
        x = following
        if i == 0:
            pl.semaphore_wait(barrier, jnp.minimum(t, reach) + n_sec - odd)
            for k in range(1, n_sec):
                users_copy(k).start()
            for d in range(reach, 0, -1):

                @pl.when(t >= d)
                def _(d=d):
                    cnt_copy(d).start()

    last = parts - 1
    taken = second_product(last, active, slice(0, crossing)) + acc[:crossing]
    pair_send[...] = taken.astype(BF16)
    pair_copy().start()
    kept = second_product(last, active, slice(crossing, held))
    acc[crossing:] = acc[crossing:] + kept
    pair_copy().wait_recv()

    @pl.when(odd == 1)
    def _():
        acc[crossing + sess :] += pair_recv[...].astype(F32)

    @pl.when(odd == 0)
    def _():
        acc[crossing : crossing + crossing] += pair_recv[...].astype(F32)

    for j in range(half, 0, -1):

        @pl.when(t >= 2 * j)
        def _(j=j):
            first = crossing + j * sess
            sums_send[j - 1] = acc[first : first + sess].astype(BF16)
            sums_copy(j).start()

    cnt_row = cnt_send.at[0]
    for d in range(1, reach + 1):

        @pl.when(t + d < n_tm)
        def _(d=d):
            cnt_copy(d).wait_recv()
            cnt_row[...] += cnt_recv[d - 1]

    count = jnp.sum(
        jnp.where(diagonal, cnt_row[:1], 0.0), axis=1, keepdims=True
    )
    share = 0.5 / jnp.maximum(count, 1.0)
    embedded = jnp.log(1.0 + count) * embed_v[...]
    for j in range(1, half + 1):

        @pl.when(t + 2 * j < n_tm)
        def _(j=j):
            sums_copy(j).wait_recv()
            acc[crossing : crossing + sess] += sums_recv[j - 1].astype(F32)

    mixed = acc[crossing : crossing + sess] * share + embedded
    mean = jnp.mean(mixed * mixed, axis=1, keepdims=True)
    rows = (mixed * lax.rsqrt(mean + 1e-06) * gain_v[...]).astype(BF16)
    outgoing = jnp.dot(place, rows, preferred_element_type=F32).astype(BF16)
    rows_send[...] = outgoing.reshape(n_sec, padded, width)
    for k in range(1, n_sec):
        rows_copy(k).start()
    rows_recv[u] = rows_send[u]
    users_recv[u] = users_send[u]

    for k in range(1, n_sec):
        users_copy(k).wait_recv()
    out_users[0] = jnp.sum(users_recv[...], axis=0)[:1] - 1
    pair_copy().wait_send()
    for d in range(1, reach + 1):

        @pl.when(t >= d)
        def _(d=d):
            cnt_copy(d).wait_send()

    for j in range(1, half + 1):

        @pl.when(t >= 2 * j)
        def _(j=j):
            sums_copy(j).wait_send()

    for k in range(1, n_sec):
        users_copy(k).wait_send()
        rows_copy(k).wait_send()
    for k in range(1, n_sec):
        rows_copy(k).wait_recv()
    if padded == cap:
        out_rows[0, 0] = rows_recv[...].reshape(slots, width)
    else:
        whole = rows_recv[...].astype(F32)[:, :cap]
        out_rows[0, 0] = whole.reshape(slots, width).astype(BF16)


def on_device(
    n_tm,
    n_sec,
    events,
    w_first,
    b_first,
    w_second,
    count_embed,
    norm_gain,
    event_session,
    event_count,
    session_user,
):
    _, ev_rows, width = events.shape
    hidden = w_first.shape[1]
    sess = session_user.shape[1]
    reach = n_tm // 2
    cap = max(2, 2 * sess // n_sec)
    padded = -(-cap // 16) * 16
    slots = n_sec * cap
    held = (reach + 1) * sess
    half = reach // 2
    parts = hidden // min(256, hidden)
    dma = pltpu.SemaphoreType.DMA
    vmem = pl.BlockSpec(memory_space=pltpu.VMEM)
    hbm = pl.BlockSpec(memory_space=pl.ANY)
    return pl.pallas_call(
        functools.partial(kernel, n_tm, n_sec, reach, cap),
        out_shape=(
            jax.ShapeDtypeStruct((1, 1, slots, width), BF16),
            jax.ShapeDtypeStruct((1, 1, slots), I32),
        ),
        in_specs=[hbm] * 9,
        out_specs=(vmem, vmem),
        scratch_shapes=[
            pltpu.VMEM((ev_rows, width), BF16),
            pltpu.VMEM((width, hidden), BF16),
            pltpu.VMEM((hidden, width), BF16),
            pltpu.VMEM((1, hidden), F32),
            pltpu.VMEM((1, width), F32),
            pltpu.VMEM((1, width), F32),
            pltpu.VMEM((1, ev_rows), I32),
            pltpu.VMEM((1, 1), I32),
            pltpu.VMEM((1, sess), I32),
            pltpu.VMEM((held, width), F32),
            pltpu.VMEM((reach + 1, 8, 128), F32),
            pltpu.VMEM((reach, 8, 128), F32),
            pltpu.VMEM((half * sess, width), BF16),
            pltpu.VMEM((half * sess, width), BF16),
            pltpu.VMEM((half, sess, width), BF16),
            pltpu.VMEM((half, sess, width), BF16),
            pltpu.VMEM((n_sec, padded, width), BF16),
            pltpu.VMEM((n_sec, padded, width), BF16),
            pltpu.VMEM((n_sec, 8, slots), I32),
            pltpu.VMEM((n_sec, 8, slots), I32),
            dma((6,)),
            dma,
            dma((parts,)),
            dma((parts,)),
            dma((2,)),
            dma((half,)),
            dma((half,)),
            dma((reach,)),
            dma((reach,)),
            dma((n_sec - 1,)),
            dma((n_sec - 1,)),
            dma((n_sec - 1,)),
            dma((n_sec - 1,)),
        ],
        compiler_params=pltpu.CompilerParams(
            collective_id=0, has_side_effects=True, vmem_limit_bytes=VMEM_BYTES
        ),
        name="pool_and_route",
    )(
        events,
        w_first,
        w_second,
        b_first.reshape(1, hidden),
        count_embed.reshape(1, width),
        norm_gain.reshape(1, width),
        event_session,
        event_count,
        session_user,
    )


def solution(mesh):
    in_specs = (
        P("user", "tm", None),
        P(),
        P(),
        P(),
        P(),
        P(),
        P("user", "tm"),
        P("user", "tm"),
        P("user", "tm"),
    )
    out_specs = (P("tm", "user", None, None), P("tm", "user", None))
    return jax.shard_map(
        functools.partial(on_device, mesh.shape["tm"], mesh.shape["user"]),
        mesh=mesh,
        in_specs=in_specs,
        out_specs=out_specs,
        check_vma=False,
    )
```

```python
import functools
import math

import jax
import jax.numpy as jnp
from jax import lax
from jax.experimental import pallas as pl
from jax.experimental.pallas import tpu as pltpu
from jax.sharding import PartitionSpec as P

MESH = pl.DeviceIdType.MESH
BF16 = jnp.bfloat16
F32 = jnp.float32
I32 = jnp.int32
VMEM_BYTES = 63 << 20


def iota(shape, axis):
    return lax.broadcasted_iota(I32, shape, axis)


def kernel(
    n_tm,
    n_sec,
    reach,
    cap,
    events,
    w_first,
    w_second,
    b_first,
    count_embed,
    norm_gain,
    event_session,
    event_count,
    session_user,
    out_rows,
    out_users,
    ev_v,
    w1_v,
    w2_v,
    b1_v,
    embed_v,
    gain_v,
    ids_v,
    count_v,
    user_v,
    acc,
    cnt_send,
    cnt_recv,
    sums_send,
    sums_recv,
    rows_send,
    rows_recv,
    users_send,
    users_recv,
    small_sem,
    ev_sem,
    w1_sem,
    w2_sem,
    sums_ss,
    sums_rs,
    cnt_ss,
    cnt_rs,
    rows_ss,
    rows_rs,
    users_ss,
    users_rs,
):
    t = lax.axis_index("tm")
    u = lax.axis_index("user")
    ev_rows, width = ev_v.shape
    hidden = w1_v.shape[1]
    sess = user_v.shape[1]
    held = (reach + 1) * sess
    step = min(256, hidden)
    parts = hidden // step

    def load(src, dst, sem):
        copy = pltpu.make_async_copy(src, dst, sem)
        copy.start()
        return copy

    small = [
        load(src, dst, small_sem.at[i])
        for i, (src, dst) in enumerate(
            (
                (event_session, ids_v),
                (event_count, count_v),
                (session_user, user_v),
                (b_first, b1_v),
                (count_embed, embed_v),
                (norm_gain, gain_v),
            )
        )
    ]
    w1_load, w2_load = [], []
    for i in range(parts):
        cols = pl.ds(i * step, step)
        w1_load.append(load(w_first.at[:, cols], w1_v.at[:, cols], w1_sem.at[i]))
        if i == 0:
            ev_load = load(events.at[0], ev_v, ev_sem)
    for i in range(parts):
        cols = pl.ds(i * step, step)
        w2_load.append(load(w_second.at[cols], w2_v.at[cols], w2_sem.at[i]))

    barrier = pltpu.get_barrier_semaphore()

    def greet(device):
        pl.semaphore_signal(barrier, inc=1, device_id=device, device_id_type=MESH)

    for d in range(1, reach + 1):

        @pl.when(t + d < n_tm)
        def _(d=d):
            greet({"tm": t + d})

    for k in range(1, n_sec):
        greet({"user": lax.rem(u + k, n_sec)})

    def sums_copy(d):
        return pltpu.make_async_remote_copy(
            src_ref=sums_send.at[reach - d],
            dst_ref=sums_recv.at[d - 1],
            send_sem=sums_ss.at[d - 1],
            recv_sem=sums_rs.at[d - 1],
            device_id={"tm": t - d},
            device_id_type=MESH,
        )

    def cnt_copy(d):
        return pltpu.make_async_remote_copy(
            src_ref=cnt_send.at[d],
            dst_ref=cnt_recv.at[d - 1],
            send_sem=cnt_ss.at[d - 1],
            recv_sem=cnt_rs.at[d - 1],
            device_id={"tm": t - d},
            device_id_type=MESH,
        )

    def routed_copy(k, send, recv, ss, rs):
        v = lax.rem(u + k, n_sec)
        return pltpu.make_async_remote_copy(
            src_ref=send.at[v],
            dst_ref=recv.at[u],
            send_sem=ss.at[k - 1],
            recv_sem=rs.at[k - 1],
            device_id={"user": v},
            device_id_type=MESH,
        )

    def rows_copy(k):
        return routed_copy(k, rows_send, rows_recv, rows_ss, rows_rs)

    def users_copy(k):
        return routed_copy(k, users_send, users_recv, users_ss, users_rs)

    c_one = math.sqrt(2.0 / math.pi)
    c_three = c_one * 0.044715

    def activated(i):
        cols = slice(i * step, (i + 1) * step)
        tiles = []
        for first in range(0, ev_rows, 256):
            x = jnp.dot(
                ev_v[first : first + 256],
                w1_v[:, cols],
                preferred_element_type=F32,
            )
            x = x + b1_v[:, cols]
            twice = x + x * jnp.tanh(x * (c_one + c_three * (x * x)))
            tiles.append(twice.astype(BF16))
        return jnp.concatenate(tiles, axis=0)

    def second_product(i, active, rows):
        cols = slice(i * step, (i + 1) * step)
        pooled = jnp.dot(assign[rows], active, preferred_element_type=F32)
        return jnp.dot(pooled.astype(BF16), w2_v[cols, :], preferred_element_type=F32)

    for copy in small:
        copy.wait()
    w1_load[0].wait()
    ev_load.wait()
    active = activated(0)

    ids = ids_v[...]
    local = ids - (t - reach) * sess
    lane = iota((1, ev_rows), 1)
    local = jnp.where(lane < count_v[...], local, -1)
    belongs = jnp.where(local == iota((held, ev_rows), 0), 1.0, 0.0)
    assign = belongs.astype(BF16)

    for copy in w1_load[1:] + w2_load:
        copy.wait()
    far = (reach + 1) // 2 * sess
    total = second_product(0, active, slice(0, held))
    for i in range(1, parts - 1):
        total = total + second_product(i, activated(i), slice(0, held))
    active = activated(parts - 1)
    first_half = total[:far] + second_product(parts - 1, active, slice(0, far))
    sums_send[: far // sess] = first_half.reshape(-1, sess, width).astype(BF16)

    pl.semaphore_wait(barrier, jnp.minimum(t, reach) + n_sec - 1)

    def send_sums(d):
        @pl.when(t >= d)
        def _():
            sums_copy(d).start()

    for d in range(reach, reach - far // sess, -1):
        send_sums(d)
    rest = total[far:] + second_product(parts - 1, active, slice(far, held))
    near = rest[: held - far - sess]
    sums_send[far // sess :] = near.reshape(-1, sess, width).astype(BF16)
    for d in range(reach - far // sess, 0, -1):
        send_sums(d)
    acc[...] = rest[held - far - sess :]

    totals = jnp.sum(belongs, axis=1, keepdims=True)
    diagonal = iota((sess, 128), 0) == iota((sess, 128), 1)
    for d in range(reach + 1):
        first = (reach - d) * sess
        as_row = jnp.where(diagonal, totals[first : first + sess], 0.0)
        cnt_send[d] = jnp.broadcast_to(
            jnp.sum(as_row, axis=0, keepdims=True), (8, 128)
        )
    for d in range(reach, 0, -1):

        @pl.when(t >= d)
        def _(d=d):
            cnt_copy(d).start()

    user_row = user_v[...]
    square = iota((sess, sess), 0), iota((sess, sess), 1)
    user_col = jnp.sum(
        jnp.where(square[0] == square[1], user_row, 0), axis=1, keepdims=True
    )
    sec_row = lax.rem(user_row, n_sec)
    sec_col = lax.rem(user_col, n_sec)
    same = jnp.where(sec_row == sec_col, 1, 0)
    rank_row = jnp.sum(
        jnp.where(square[0] < square[1], same, 0), axis=0, keepdims=True
    )
    rank_col = jnp.sum(
        jnp.where(square[1] < square[0], same, 0), axis=1, keepdims=True
    )
    padded = rows_send.shape[1]
    place = jnp.where(
        sec_row * padded + rank_row == iota((n_sec * padded, sess), 0), 1.0, 0.0
    ).astype(BF16)
    slots = n_sec * cap
    at = iota((sess, slots), 1) == rank_col + u * cap
    for v in range(n_sec):
        named = jnp.where(at & (sec_col == v), user_col + 1, 0)
        users_send[v] = jnp.broadcast_to(
            jnp.sum(named, axis=0, keepdims=True), (8, slots)
        )
    for k in range(1, n_sec):
        users_copy(k).start()
    users_recv[u] = users_send[u]

    for d in range(1, reach + 1):

        @pl.when(t + d < n_tm)
        def _(d=d):
            cnt_copy(d).wait_recv()
            cnt_send[0] += cnt_recv[d - 1]

    count = jnp.sum(
        jnp.where(diagonal, cnt_send[0][:1], 0.0), axis=1, keepdims=True
    )
    share = 0.5 / jnp.maximum(count, 1.0)
    embedded = jnp.log(1.0 + count) * embed_v[...]
    for k in range(1, n_sec):
        users_copy(k).wait_recv()
    out_users[0] = jnp.sum(users_recv[...], axis=0)[:1] - 1

    for d in range(1, reach + 1):

        @pl.when(t + d < n_tm)
        def _(d=d):
            sums_copy(d).wait_recv()
            acc[...] += sums_recv[d - 1].astype(F32)

    mixed = acc[...] * share + embedded
    mean = jnp.mean(mixed * mixed, axis=1, keepdims=True)
    rows = (mixed * lax.rsqrt(mean + 1e-06) * gain_v[...]).astype(BF16)
    outgoing = jnp.dot(place, rows, preferred_element_type=F32).astype(BF16)
    rows_send[...] = outgoing.reshape(n_sec, padded, width)
    for k in range(1, n_sec):
        rows_copy(k).start()
    rows_recv[u] = rows_send[u]

    for d in range(1, reach + 1):

        @pl.when(t >= d)
        def _(d=d):
            cnt_copy(d).wait_send()
            sums_copy(d).wait_send()

    for k in range(1, n_sec):
        users_copy(k).wait_send()
        rows_copy(k).wait_send()
    for k in range(1, n_sec):
        rows_copy(k).wait_recv()
    if padded == cap:
        out_rows[0, 0] = rows_recv[...].reshape(slots, width)
    else:
        whole = rows_recv[...].astype(F32)[:, :cap]
        out_rows[0, 0] = whole.reshape(slots, width).astype(BF16)


def on_device(
    n_tm,
    n_sec,
    events,
    w_first,
    b_first,
    w_second,
    count_embed,
    norm_gain,
    event_session,
    event_count,
    session_user,
):
    _, ev_rows, width = events.shape
    hidden = w_first.shape[1]
    sess = session_user.shape[1]
    reach = n_tm // 2
    cap = max(2, 2 * sess // n_sec)
    padded = -(-cap // 16) * 16
    slots = n_sec * cap
    parts = hidden // min(256, hidden)
    dma = pltpu.SemaphoreType.DMA
    vmem = pl.BlockSpec(memory_space=pltpu.VMEM)
    hbm = pl.BlockSpec(memory_space=pl.ANY)
    return pl.pallas_call(
        functools.partial(kernel, n_tm, n_sec, reach, cap),
        out_shape=(
            jax.ShapeDtypeStruct((1, 1, slots, width), BF16),
            jax.ShapeDtypeStruct((1, 1, slots), I32),
        ),
        in_specs=[hbm] * 9,
        out_specs=(vmem, vmem),
        scratch_shapes=[
            pltpu.VMEM((ev_rows, width), BF16),
            pltpu.VMEM((width, hidden), BF16),
            pltpu.VMEM((hidden, width), BF16),
            pltpu.VMEM((1, hidden), F32),
            pltpu.VMEM((1, width), F32),
            pltpu.VMEM((1, width), F32),
            pltpu.VMEM((1, ev_rows), I32),
            pltpu.VMEM((1, 1), I32),
            pltpu.VMEM((1, sess), I32),
            pltpu.VMEM((sess, width), F32),
            pltpu.VMEM((reach + 1, 8, 128), F32),
            pltpu.VMEM((reach, 8, 128), F32),
            pltpu.VMEM((reach, sess, width), BF16),
            pltpu.VMEM((reach, sess, width), BF16),
            pltpu.VMEM((n_sec, padded, width), BF16),
            pltpu.VMEM((n_sec, padded, width), BF16),
            pltpu.VMEM((n_sec, 8, slots), I32),
            pltpu.VMEM((n_sec, 8, slots), I32),
            dma((6,)),
            dma,
            dma((parts,)),
            dma((parts,)),
            dma((reach,)),
            dma((reach,)),
            dma((reach,)),
            dma((reach,)),
            dma((n_sec - 1,)),
            dma((n_sec - 1,)),
            dma((n_sec - 1,)),
            dma((n_sec - 1,)),
        ],
        compiler_params=pltpu.CompilerParams(
            collective_id=0, has_side_effects=True, vmem_limit_bytes=VMEM_BYTES
        ),
        name="pool_and_route",
    )(
        events,
        w_first,
        w_second,
        b_first.reshape(1, hidden),
        count_embed.reshape(1, width),
        norm_gain.reshape(1, width),
        event_session,
        event_count,
        session_user,
    )


def solution(mesh):
    in_specs = (
        P("user", "tm", None),
        P(),
        P(),
        P(),
        P(),
        P(),
        P("user", "tm"),
        P("user", "tm"),
        P("user", "tm"),
    )
    out_specs = (P("tm", "user", None, None), P("tm", "user", None))
    return jax.shard_map(
        functools.partial(on_device, mesh.shape["tm"], mesh.shape["user"]),
        mesh=mesh,
        in_specs=in_specs,
        out_specs=out_specs,
        check_vma=False,
    )
```

```python
import functools
import math

import jax
import jax.numpy as jnp
from jax import lax
from jax.experimental import pallas as pl
from jax.experimental.pallas import tpu as pltpu
from jax.sharding import PartitionSpec as P

MESH = pl.DeviceIdType.MESH
BF16 = jnp.bfloat16
F32 = jnp.float32
I32 = jnp.int32
VMEM_BYTES = 63 << 20


def iota(shape, axis):
    return lax.broadcasted_iota(I32, shape, axis)


def kernel(
    n_tm,
    n_sec,
    reach,
    cap,
    events,
    w_first,
    w_second,
    b_first,
    count_embed,
    norm_gain,
    event_session,
    event_count,
    session_user,
    out_rows,
    out_users,
    ev_v,
    w1_v,
    w2_v,
    b1_v,
    embed_v,
    gain_v,
    ids_v,
    count_v,
    user_v,
    hid,
    acc,
    cnt_send,
    cnt_recv,
    sums_send,
    sums_recv,
    rows_send,
    rows_recv,
    users_send,
    users_recv,
    staged_rows,
    staged_users,
    small_sem,
    ev_sem,
    w1_sem,
    w2_sem,
    sums_ss,
    sums_rs,
    cnt_ss,
    cnt_rs,
    rows_ss,
    rows_rs,
    users_ss,
    users_rs,
    out_sem,
):
    t = lax.axis_index("tm")
    u = lax.axis_index("user")
    ev_rows, width = ev_v.shape
    hidden = w1_v.shape[1]
    sess = user_v.shape[1]
    held = (reach + 1) * sess
    step = min(256, hidden)
    parts = hidden // step
    padded = rows_send.shape[1]
    direct = padded == cap
    slots = n_sec * cap

    def load(src, dst, sem):
        copy = pltpu.make_async_copy(src, dst, sem)
        copy.start()
        return copy

    small = [
        load(src, dst, small_sem.at[i])
        for i, (src, dst) in enumerate(
            (
                (event_session, ids_v),
                (event_count, count_v),
                (session_user, user_v),
                (b_first, b1_v),
                (count_embed, embed_v),
                (norm_gain, gain_v),
            )
        )
    ]
    w2_load = []
    for i in range(parts):
        cols = pl.ds(i * step, step)
        load(w_first.at[:, cols], w1_v.at[:, cols], w1_sem.at[i])
        if i == 0:
            ev_load = load(events.at[0], ev_v, ev_sem)
    for i in range(parts):
        cols = pl.ds(i * step, step)
        w2_load.append(load(w_second.at[cols], w2_v.at[cols], w2_sem.at[i]))

    barrier = pltpu.get_barrier_semaphore()

    def greet(device):
        pl.semaphore_signal(barrier, inc=1, device_id=device, device_id_type=MESH)

    for d in range(1, reach + 1):

        @pl.when(t + d < n_tm)
        def _(d=d):
            greet({"tm": t + d})

    for k in range(1, n_sec):
        greet({"user": lax.rem(u + k, n_sec)})

    def sums_copy(d):
        return pltpu.make_async_remote_copy(
            src_ref=sums_send.at[reach - d],
            dst_ref=sums_recv.at[d - 1],
            send_sem=sums_ss.at[d - 1],
            recv_sem=sums_rs.at[d - 1],
            device_id={"tm": t - d},
            device_id_type=MESH,
        )

    def cnt_copy(d):
        return pltpu.make_async_remote_copy(
            src_ref=cnt_send.at[d],
            dst_ref=cnt_recv.at[d - 1],
            send_sem=cnt_ss.at[d - 1],
            recv_sem=cnt_rs.at[d - 1],
            device_id={"tm": t - d},
            device_id_type=MESH,
        )

    def rows_copy(k):
        v = lax.rem(u + k, n_sec)
        return pltpu.make_async_remote_copy(
            src_ref=rows_send.at[v],
            dst_ref=landing(),
            send_sem=rows_ss.at[k - 1],
            recv_sem=rows_rs.at[k - 1],
            device_id={"user": v},
            device_id_type=MESH,
        )

    def landing():
        if direct:
            return out_rows.at[0, 0, pl.ds(pl.multiple_of(u * cap, cap), cap)]
        return rows_recv.at[u]

    def users_copy(k):
        v = lax.rem(u + k, n_sec)
        return pltpu.make_async_remote_copy(
            src_ref=users_send.at[v],
            dst_ref=users_recv.at[u],
            send_sem=users_ss.at[k - 1],
            recv_sem=users_rs.at[k - 1],
            device_id={"user": v},
            device_id_type=MESH,
        )

    c_one = math.sqrt(2.0 / math.pi)
    c_three = c_one * 0.044715

    def columns(i):
        if isinstance(i, int):
            return pl.ds(i * step, step)
        return pl.ds(pl.multiple_of(i * step, step), step)

    def activate(i):
        cols = columns(i)
        pltpu.make_async_copy(
            w_first.at[:, cols], w1_v.at[:, cols], w1_sem.at[i]
        ).wait()
        slot = lax.rem(i, 2)
        for first in range(0, ev_rows, 256):
            x = jnp.dot(
                ev_v[first : first + 256],
                w1_v[:, cols],
                preferred_element_type=F32,
            )
            x = x + b1_v[:, cols]
            twice = x + x * jnp.tanh(x * (c_one + c_three * (x * x)))
            hid[slot, first : first + 256] = twice.astype(BF16)

    def second_product(i, rows):
        active = hid[lax.rem(i, 2)]
        pooled = jnp.dot(assign[rows], active, preferred_element_type=F32)
        return jnp.dot(
            pooled.astype(BF16), w2_v[columns(i), :], preferred_element_type=F32
        )

    for copy in small:
        copy.wait()
    ev_load.wait()
    activate(0)

    ids = ids_v[...]
    local = ids - (t - reach) * sess
    lane = iota((1, ev_rows), 1)
    local = jnp.where(lane < count_v[...], local, -1)
    belongs = jnp.where(local == iota((held, ev_rows), 0), 1.0, 0.0)
    assign = belongs.astype(BF16)

    for copy in w2_load:
        copy.wait()
    far = (reach + 1) // 2 * sess
    acc[...] = jnp.zeros_like(acc)

    @pl.loop(1, parts)
    def _(i):
        activate(i)
        acc[...] += second_product(i - 1, slice(0, held))

    first_half = acc[:far] + second_product(parts - 1, slice(0, far))
    sums_send[: far // sess] = first_half.reshape(-1, sess, width).astype(BF16)

    pl.semaphore_wait(barrier, jnp.minimum(t, reach) + n_sec - 1)

    def send_sums(d):
        @pl.when(t >= d)
        def _():
            sums_copy(d).start()

    for d in range(reach, reach - far // sess, -1):
        send_sums(d)
    rest = acc[far:] + second_product(parts - 1, slice(far, held))
    near = rest[: held - far - sess]
    sums_send[far // sess :] = near.reshape(-1, sess, width).astype(BF16)
    for d in range(reach - far // sess, 0, -1):
        send_sums(d)
    acc[:sess] = rest[held - far - sess :]

    totals = jnp.sum(belongs, axis=1, keepdims=True)
    diagonal = iota((sess, 128), 0) == iota((sess, 128), 1)
    for d in range(reach + 1):
        first = (reach - d) * sess
        as_row = jnp.where(diagonal, totals[first : first + sess], 0.0)
        cnt_send[d] = jnp.broadcast_to(
            jnp.sum(as_row, axis=0, keepdims=True), (8, 128)
        )
    for d in range(reach, 0, -1):

        @pl.when(t >= d)
        def _(d=d):
            cnt_copy(d).start()

    user_row = user_v[...]
    square = iota((sess, sess), 0), iota((sess, sess), 1)
    user_col = jnp.sum(
        jnp.where(square[0] == square[1], user_row, 0), axis=1, keepdims=True
    )
    sec_row = lax.rem(user_row, n_sec)
    sec_col = lax.rem(user_col, n_sec)
    same = jnp.where(sec_row == sec_col, 1, 0)
    rank_row = jnp.sum(
        jnp.where(square[0] < square[1], same, 0), axis=0, keepdims=True
    )
    rank_col = jnp.sum(
        jnp.where(square[1] < square[0], same, 0), axis=1, keepdims=True
    )
    place = jnp.where(
        sec_row * padded + rank_row == iota((n_sec * padded, sess), 0), 1.0, 0.0
    ).astype(BF16)
    at = iota((sess, slots), 1) == rank_col + u * cap
    for v in range(n_sec):
        named = jnp.where(at & (sec_col == v), user_col + 1, 0)
        users_send[v] = jnp.broadcast_to(
            jnp.sum(named, axis=0, keepdims=True), (8, slots)
        )
    for k in range(1, n_sec):
        users_copy(k).start()
    users_recv[u] = users_send[u]

    for d in range(1, reach + 1):

        @pl.when(t + d < n_tm)
        def _(d=d):
            cnt_copy(d).wait_recv()
            cnt_send[0] += cnt_recv[d - 1]

    count = jnp.sum(
        jnp.where(diagonal, cnt_send[0][:1], 0.0), axis=1, keepdims=True
    )
    share = 0.5 / jnp.maximum(count, 1.0)
    embedded = jnp.log(1.0 + count) * embed_v[...]
    for k in range(1, n_sec):
        users_copy(k).wait_recv()
    staged_users[...] = jnp.sum(users_recv[...], axis=0)[:1] - 1
    users_out = load(staged_users, out_users.at[0], out_sem.at[0])

    for d in range(1, reach + 1):

        @pl.when(t + d < n_tm)
        def _(d=d):
            sums_copy(d).wait_recv()
            acc[:sess] += sums_recv[d - 1].astype(F32)

    mixed = acc[:sess] * share + embedded
    mean = jnp.mean(mixed * mixed, axis=1, keepdims=True)
    rows = (mixed * lax.rsqrt(mean + 1e-06) * gain_v[...]).astype(BF16)
    outgoing = jnp.dot(place, rows, preferred_element_type=F32).astype(BF16)
    rows_send[...] = outgoing.reshape(n_sec, padded, width)
    for k in range(1, n_sec):
        rows_copy(k).start()
    if direct:
        own = load(rows_send.at[u], landing(), out_sem.at[1])
    else:
        rows_recv[u] = rows_send[u]

    for d in range(1, reach + 1):

        @pl.when(t >= d)
        def _(d=d):
            cnt_copy(d).wait_send()
            sums_copy(d).wait_send()

    for k in range(1, n_sec):
        users_copy(k).wait_send()
        rows_copy(k).wait_send()
    for k in range(1, n_sec):
        rows_copy(k).wait_recv()
    if direct:
        own.wait()
    else:
        whole = rows_recv[...].astype(F32)[:, :cap]
        staged_rows[...] = whole.reshape(slots, width).astype(BF16)
        load(staged_rows, out_rows.at[0, 0], out_sem.at[1]).wait()
    users_out.wait()


def hand_over(rows_in, users_in, rows_out, users_out, sem):
    slots = rows_in.shape[2]
    pieces = 4 if slots % 64 == 0 else 1
    size = slots // pieces
    copies = [pltpu.make_async_copy(users_in, users_out, sem.at[pieces])]
    for i in range(pieces):
        piece = (0, 0, pl.ds(i * size, size))
        copies.append(
            pltpu.make_async_copy(rows_in.at[piece], rows_out.at[piece], sem.at[i])
        )
    for copy in copies:
        copy.start()
    for copy in copies:
        copy.wait()


def on_device(
    n_tm,
    n_sec,
    events,
    w_first,
    b_first,
    w_second,
    count_embed,
    norm_gain,
    event_session,
    event_count,
    session_user,
):
    _, ev_rows, width = events.shape
    hidden = w_first.shape[1]
    sess = session_user.shape[1]
    reach = n_tm // 2
    cap = max(2, 2 * sess // n_sec)
    padded = -(-cap // 16) * 16
    slots = n_sec * cap
    parts = hidden // min(256, hidden)
    dma = pltpu.SemaphoreType.DMA
    hbm = pl.BlockSpec(memory_space=pl.ANY)
    out_shape = (
        jax.ShapeDtypeStruct((1, 1, slots, width), BF16),
        jax.ShapeDtypeStruct((1, 1, slots), I32),
    )
    routed = pl.pallas_call(
        functools.partial(kernel, n_tm, n_sec, reach, cap),
        out_shape=out_shape,
        in_specs=[hbm] * 9,
        out_specs=(hbm, hbm),
        scratch_shapes=[
            pltpu.VMEM((ev_rows, width), BF16),
            pltpu.VMEM((width, hidden), BF16),
            pltpu.VMEM((hidden, width), BF16),
            pltpu.VMEM((1, hidden), F32),
            pltpu.VMEM((1, width), F32),
            pltpu.VMEM((1, width), F32),
            pltpu.VMEM((1, ev_rows), I32),
            pltpu.VMEM((1, 1), I32),
            pltpu.VMEM((1, sess), I32),
            pltpu.VMEM((2, ev_rows, hidden // parts), BF16),
            pltpu.VMEM(((reach + 1) * sess, width), F32),
            pltpu.VMEM((reach + 1, 8, 128), F32),
            pltpu.VMEM((reach, 8, 128), F32),
            pltpu.VMEM((reach, sess, width), BF16),
            pltpu.VMEM((reach, sess, width), BF16),
            pltpu.VMEM((n_sec, padded, width), BF16),
            pltpu.VMEM((n_sec, padded, width), BF16),
            pltpu.VMEM((n_sec, 8, slots), I32),
            pltpu.VMEM((n_sec, 8, slots), I32),
            pltpu.VMEM((slots, width), BF16),
            pltpu.VMEM((1, slots), I32),
            dma((6,)),
            dma,
            dma((parts,)),
            dma((parts,)),
            dma((reach,)),
            dma((reach,)),
            dma((reach,)),
            dma((reach,)),
            dma((n_sec - 1,)),
            dma((n_sec - 1,)),
            dma((n_sec - 1,)),
            dma((n_sec - 1,)),
            dma((2,)),
        ],
        compiler_params=pltpu.CompilerParams(
            collective_id=0, has_side_effects=True, vmem_limit_bytes=VMEM_BYTES
        ),
        name="pool_and_route",
    )(
        events,
        w_first,
        w_second,
        b_first.reshape(1, hidden),
        count_embed.reshape(1, width),
        norm_gain.reshape(1, width),
        event_session,
        event_count,
        session_user,
    )
    return pl.pallas_call(
        hand_over,
        out_shape=out_shape,
        in_specs=[hbm] * 2,
        out_specs=(hbm, hbm),
        scratch_shapes=[dma((5,))],
        compiler_params=pltpu.CompilerParams(vmem_limit_bytes=VMEM_BYTES),
        name="hand_over",
    )(*routed)


def solution(mesh):
    in_specs = (
        P("user", "tm", None),
        P(),
        P(),
        P(),
        P(),
        P(),
        P("user", "tm"),
        P("user", "tm"),
        P("user", "tm"),
    )
    out_specs = (P("tm", "user", None, None), P("tm", "user", None))
    return jax.shard_map(
        functools.partial(on_device, mesh.shape["tm"], mesh.shape["user"]),
        mesh=mesh,
        in_specs=in_specs,
        out_specs=out_specs,
        check_vma=False,
    )
```

```python
import functools
import math

import jax
import jax.numpy as jnp
from jax import lax
from jax.experimental import pallas as pl
from jax.experimental.pallas import tpu as pltpu
from jax.sharding import PartitionSpec as P

MESH = pl.DeviceIdType.MESH
BF16 = jnp.bfloat16
F32 = jnp.float32
I32 = jnp.int32
VMEM_BYTES = 48 << 20


def iota(shape, axis):
    return lax.broadcasted_iota(I32, shape, axis)


def kernel(
    n_tm,
    n_sec,
    reach,
    cap,
    events,
    w_first,
    w_second,
    b_first,
    count_embed,
    norm_gain,
    event_session,
    event_count,
    session_user,
    out_rows,
    out_users,
    ev_v,
    w1_v,
    w2_v,
    b1_v,
    embed_v,
    gain_v,
    ids_v,
    count_v,
    user_v,
    acc,
    cnt_send,
    cnt_recv,
    sums_send,
    sums_recv,
    rows_send,
    rows_recv,
    users_send,
    users_recv,
    small_sem,
    ev_sem,
    w1_sem,
    w2_sem,
    sums_ss,
    sums_rs,
    cnt_ss,
    cnt_rs,
    rows_ss,
    rows_rs,
    users_ss,
    users_rs,
):
    t = lax.axis_index("tm")
    u = lax.axis_index("user")
    ev_rows, width = ev_v.shape
    hidden = w1_v.shape[1]
    sess = user_v.shape[1]
    held = (reach + 1) * sess
    step = min(256, hidden)
    parts = hidden // step

    def load(src, dst, sem):
        copy = pltpu.make_async_copy(src, dst, sem)
        copy.start()
        return copy

    small = [
        load(src, dst, small_sem.at[i])
        for i, (src, dst) in enumerate(
            (
                (event_session, ids_v),
                (event_count, count_v),
                (session_user, user_v),
                (b_first, b1_v),
                (count_embed, embed_v),
                (norm_gain, gain_v),
            )
        )
    ]
    w1_load, w2_load = [], []
    for i in range(parts):
        cols = pl.ds(i * step, step)
        w1_load.append(load(w_first.at[:, cols], w1_v.at[:, cols], w1_sem.at[i]))
        if i == 0:
            ev_load = load(events.at[0], ev_v, ev_sem)
    for i in range(parts):
        cols = pl.ds(i * step, step)
        w2_load.append(load(w_second.at[cols], w2_v.at[cols], w2_sem.at[i]))

    barrier = pltpu.get_barrier_semaphore()

    def greet(device):
        pl.semaphore_signal(barrier, inc=1, device_id=device, device_id_type=MESH)

    for d in range(1, reach + 1):

        @pl.when(t + d < n_tm)
        def _(d=d):
            greet({"tm": t + d})

    for k in range(1, n_sec):
        greet({"user": lax.rem(u + k, n_sec)})

    def sums_copy(d):
        return pltpu.make_async_remote_copy(
            src_ref=sums_send.at[reach - d],
            dst_ref=sums_recv.at[d - 1],
            send_sem=sums_ss.at[d - 1],
            recv_sem=sums_rs.at[d - 1],
            device_id={"tm": t - d},
            device_id_type=MESH,
        )

    def cnt_copy(d):
        return pltpu.make_async_remote_copy(
            src_ref=cnt_send.at[d],
            dst_ref=cnt_recv.at[d - 1],
            send_sem=cnt_ss.at[d - 1],
            recv_sem=cnt_rs.at[d - 1],
            device_id={"tm": t - d},
            device_id_type=MESH,
        )

    def routed_copy(k, send, recv, ss, rs):
        v = lax.rem(u + k, n_sec)
        return pltpu.make_async_remote_copy(
            src_ref=send.at[v],
            dst_ref=recv.at[u],
            send_sem=ss.at[k - 1],
            recv_sem=rs.at[k - 1],
            device_id={"user": v},
            device_id_type=MESH,
        )

    def rows_copy(k):
        return routed_copy(k, rows_send, rows_recv, rows_ss, rows_rs)

    def users_copy(k):
        return routed_copy(k, users_send, users_recv, users_ss, users_rs)

    c_one = math.sqrt(2.0 / math.pi)
    c_three = c_one * 0.044715

    def activated(i):
        cols = slice(i * step, (i + 1) * step)
        tiles = []
        for first in range(0, ev_rows, 256):
            x = jnp.dot(
                ev_v[first : first + 256],
                w1_v[:, cols],
                preferred_element_type=F32,
            )
            x = x + b1_v[:, cols]
            twice = x + x * jnp.tanh(x * (c_one + c_three * (x * x)))
            tiles.append(twice.astype(BF16))
        return jnp.concatenate(tiles, axis=0)

    def second_product(i, active, rows):
        cols = slice(i * step, (i + 1) * step)
        pooled = jnp.dot(assign[rows], active, preferred_element_type=F32)
        return jnp.dot(pooled.astype(BF16), w2_v[cols, :], preferred_element_type=F32)

    for copy in small:
        copy.wait()
    w1_load[0].wait()
    ev_load.wait()
    active = activated(0)

    ids = ids_v[...]
    local = ids - (t - reach) * sess
    lane = iota((1, ev_rows), 1)
    local = jnp.where(lane < count_v[...], local, -1)
    belongs = jnp.where(local == iota((held, ev_rows), 0), 1.0, 0.0)
    assign = belongs.astype(BF16)

    for copy in w1_load[1:] + w2_load:
        copy.wait()
    far = (reach + 1) // 2 * sess
    total = second_product(0, active, slice(0, held))
    for i in range(1, parts - 1):
        total = total + second_product(i, activated(i), slice(0, held))
    active = activated(parts - 1)
    first_half = total[:far] + second_product(parts - 1, active, slice(0, far))
    sums_send[: far // sess] = first_half.reshape(-1, sess, width).astype(BF16)

    pl.semaphore_wait(barrier, jnp.minimum(t, reach) + n_sec - 1)

    def send_sums(d):
        @pl.when(t >= d)
        def _():
            sums_copy(d).start()

    for d in range(reach, reach - far // sess, -1):
        send_sums(d)
    rest = total[far:] + second_product(parts - 1, active, slice(far, held))
    near = rest[: held - far - sess]
    sums_send[far // sess :] = near.reshape(-1, sess, width).astype(BF16)
    for d in range(reach - far // sess, 0, -1):
        send_sums(d)
    acc[...] = rest[held - far - sess :]

    totals = jnp.sum(belongs, axis=1, keepdims=True)
    diagonal = iota((sess, 128), 0) == iota((sess, 128), 1)
    for d in range(reach + 1):
        first = (reach - d) * sess
        as_row = jnp.where(diagonal, totals[first : first + sess], 0.0)
        cnt_send[d] = jnp.broadcast_to(
            jnp.sum(as_row, axis=0, keepdims=True), (8, 128)
        )
    for d in range(reach, 0, -1):

        @pl.when(t >= d)
        def _(d=d):
            cnt_copy(d).start()

    user_row = user_v[...]
    square = iota((sess, sess), 0), iota((sess, sess), 1)
    user_col = jnp.sum(
        jnp.where(square[0] == square[1], user_row, 0), axis=1, keepdims=True
    )
    sec_row = lax.rem(user_row, n_sec)
    sec_col = lax.rem(user_col, n_sec)
    same = jnp.where(sec_row == sec_col, 1, 0)
    rank_row = jnp.sum(
        jnp.where(square[0] < square[1], same, 0), axis=0, keepdims=True
    )
    rank_col = jnp.sum(
        jnp.where(square[1] < square[0], same, 0), axis=1, keepdims=True
    )
    padded = rows_send.shape[1]
    place = jnp.where(
        sec_row * padded + rank_row == iota((n_sec * padded, sess), 0), 1.0, 0.0
    ).astype(BF16)
    slots = n_sec * cap
    at = iota((sess, slots), 1) == rank_col + u * cap
    for v in range(n_sec):
        named = jnp.where(at & (sec_col == v), user_col + 1, 0)
        users_send[v] = jnp.broadcast_to(
            jnp.sum(named, axis=0, keepdims=True), (8, slots)
        )
    for k in range(1, n_sec):
        users_copy(k).start()
    users_recv[u] = users_send[u]

    for d in range(1, reach + 1):

        @pl.when(t + d < n_tm)
        def _(d=d):
            cnt_copy(d).wait_recv()
            cnt_send[0] += cnt_recv[d - 1]

    count = jnp.sum(
        jnp.where(diagonal, cnt_send[0][:1], 0.0), axis=1, keepdims=True
    )
    share = 0.5 / jnp.maximum(count, 1.0)
    embedded = jnp.log(1.0 + count) * embed_v[...]
    for k in range(1, n_sec):
        users_copy(k).wait_recv()
    out_users[0] = jnp.sum(users_recv[...], axis=0)[:1] - 1

    for d in range(1, reach + 1):

        @pl.when(t + d < n_tm)
        def _(d=d):
            sums_copy(d).wait_recv()
            acc[...] += sums_recv[d - 1].astype(F32)

    mixed = acc[...] * share + embedded
    mean = jnp.mean(mixed * mixed, axis=1, keepdims=True)
    rows = (mixed * lax.rsqrt(mean + 1e-06) * gain_v[...]).astype(BF16)
    outgoing = jnp.dot(place, rows, preferred_element_type=F32).astype(BF16)
    rows_send[...] = outgoing.reshape(n_sec, padded, width)
    for k in range(1, n_sec):
        rows_copy(k).start()
    rows_recv[u] = rows_send[u]

    for d in range(1, reach + 1):

        @pl.when(t >= d)
        def _(d=d):
            cnt_copy(d).wait_send()
            sums_copy(d).wait_send()

    for k in range(1, n_sec):
        users_copy(k).wait_send()
        rows_copy(k).wait_send()
    for k in range(1, n_sec):
        rows_copy(k).wait_recv()
    if padded == cap:
        out_rows[0, 0] = rows_recv[...].reshape(slots, width)
    else:
        whole = rows_recv[...].astype(F32)[:, :cap]
        out_rows[0, 0] = whole.reshape(slots, width).astype(BF16)


def on_device(
    n_tm,
    n_sec,
    events,
    w_first,
    b_first,
    w_second,
    count_embed,
    norm_gain,
    event_session,
    event_count,
    session_user,
):
    _, ev_rows, width = events.shape
    hidden = w_first.shape[1]
    sess = session_user.shape[1]
    reach = n_tm // 2
    cap = max(2, 2 * sess // n_sec)
    padded = -(-cap // 16) * 16
    slots = n_sec * cap
    parts = hidden // min(256, hidden)
    dma = pltpu.SemaphoreType.DMA
    vmem = pl.BlockSpec(memory_space=pltpu.VMEM)
    hbm = pl.BlockSpec(memory_space=pl.ANY)
    return pl.pallas_call(
        functools.partial(kernel, n_tm, n_sec, reach, cap),
        out_shape=(
            pltpu.VMEM((1, 1, slots, width), BF16),
            pltpu.VMEM((1, 1, slots), I32),
        ),
        in_specs=[hbm] * 9,
        out_specs=(vmem, vmem),
        scratch_shapes=[
            pltpu.VMEM((ev_rows, width), BF16),
            pltpu.VMEM((width, hidden), BF16),
            pltpu.VMEM((hidden, width), BF16),
            pltpu.VMEM((1, hidden), F32),
            pltpu.VMEM((1, width), F32),
            pltpu.VMEM((1, width), F32),
            pltpu.VMEM((1, ev_rows), I32),
            pltpu.VMEM((1, 1), I32),
            pltpu.VMEM((1, sess), I32),
            pltpu.VMEM((sess, width), F32),
            pltpu.VMEM((reach + 1, 8, 128), F32),
            pltpu.VMEM((reach, 8, 128), F32),
            pltpu.VMEM((reach, sess, width), BF16),
            pltpu.VMEM((reach, sess, width), BF16),
            pltpu.VMEM((n_sec, padded, width), BF16),
            pltpu.VMEM((n_sec, padded, width), BF16),
            pltpu.VMEM((n_sec, 8, slots), I32),
            pltpu.VMEM((n_sec, 8, slots), I32),
            dma((6,)),
            dma,
            dma((parts,)),
            dma((parts,)),
            dma((reach,)),
            dma((reach,)),
            dma((reach,)),
            dma((reach,)),
            dma((n_sec - 1,)),
            dma((n_sec - 1,)),
            dma((n_sec - 1,)),
            dma((n_sec - 1,)),
        ],
        compiler_params=pltpu.CompilerParams(
            collective_id=0, has_side_effects=True, vmem_limit_bytes=VMEM_BYTES
        ),
        name="pool_and_route",
    )(
        *(
            operand
            if operand.size == 1
            else pltpu.with_memory_space_constraint(operand, pltpu.HBM)
            for operand in (
                events,
                w_first,
                w_second,
                b_first.reshape(1, hidden),
                count_embed.reshape(1, width),
                norm_gain.reshape(1, width),
                event_session,
                event_count,
                session_user,
            )
        )
    )


def solution(mesh):
    in_specs = (
        P("user", "tm", None),
        P(),
        P(),
        P(),
        P(),
        P(),
        P("user", "tm"),
        P("user", "tm"),
        P("user", "tm"),
    )
    out_specs = (P("tm", "user", None, None), P("tm", "user", None))
    return jax.shard_map(
        functools.partial(on_device, mesh.shape["tm"], mesh.shape["user"]),
        mesh=mesh,
        in_specs=in_specs,
        out_specs=out_specs,
        check_vma=False,
    )
```

```python
import functools
import math

import jax
import jax.numpy as jnp
from jax import lax
from jax.experimental import pallas as pl
from jax.experimental.pallas import tpu as pltpu
from jax.sharding import PartitionSpec as P

MESH = pl.DeviceIdType.MESH
BF16 = jnp.bfloat16
F32 = jnp.float32
I32 = jnp.int32
VMEM_BYTES = 48 << 20


def iota(shape, axis):
    return lax.broadcasted_iota(I32, shape, axis)


def kernel(
    n_tm,
    n_sec,
    reach,
    cap,
    events,
    w_first,
    w_second,
    b_first,
    count_embed,
    norm_gain,
    event_session,
    event_count,
    session_user,
    out_rows,
    out_users,
    ev_v,
    w1_v,
    w2_v,
    b1_v,
    embed_v,
    gain_v,
    ids_v,
    count_v,
    user_v,
    acc,
    cnt_send,
    cnt_recv,
    sums_send,
    sums_recv,
    rows_send,
    rows_recv,
    users_send,
    users_recv,
    small_sem,
    ev_sem,
    w1_sem,
    w2_sem,
    sums_ss,
    sums_rs,
    cnt_ss,
    cnt_rs,
    rows_ss,
    rows_rs,
    users_ss,
    users_rs,
):
    t = lax.axis_index("tm")
    u = lax.axis_index("user")
    ev_rows, width = ev_v.shape
    hidden = w1_v.shape[1]
    sess = user_v.shape[1]
    held = (reach + 1) * sess
    step = min(256, hidden)
    parts = hidden // step
    padded = rows_send.shape[1]
    direct = padded == cap
    slots = n_sec * cap

    def load(src, dst, sem):
        copy = pltpu.make_async_copy(src, dst, sem)
        copy.start()
        return copy

    small = [
        load(src, dst, small_sem.at[i])
        for i, (src, dst) in enumerate(
            (
                (event_session, ids_v),
                (event_count, count_v),
                (session_user, user_v),
                (b_first, b1_v),
                (count_embed, embed_v),
                (norm_gain, gain_v),
            )
        )
    ]
    w1_load, w2_load = [], []
    for i in range(parts):
        cols = pl.ds(i * step, step)
        w1_load.append(load(w_first.at[:, cols], w1_v.at[:, cols], w1_sem.at[i]))
        if i == 0:
            ev_load = load(events.at[0], ev_v, ev_sem)
    for i in range(parts):
        cols = pl.ds(i * step, step)
        w2_load.append(load(w_second.at[cols], w2_v.at[cols], w2_sem.at[i]))

    barrier = pltpu.get_barrier_semaphore()

    def greet(device):
        pl.semaphore_signal(barrier, inc=1, device_id=device, device_id_type=MESH)

    for d in range(1, reach + 1):

        @pl.when(t + d < n_tm)
        def _(d=d):
            greet({"tm": t + d})

    for k in range(1, n_sec):
        greet({"user": lax.rem(u + k, n_sec)})

    def sums_copy(d):
        return pltpu.make_async_remote_copy(
            src_ref=sums_send.at[reach - d],
            dst_ref=sums_recv.at[d - 1],
            send_sem=sums_ss.at[d - 1],
            recv_sem=sums_rs.at[d - 1],
            device_id={"tm": t - d},
            device_id_type=MESH,
        )

    def cnt_copy(d):
        return pltpu.make_async_remote_copy(
            src_ref=cnt_send.at[d],
            dst_ref=cnt_recv.at[d - 1],
            send_sem=cnt_ss.at[d - 1],
            recv_sem=cnt_rs.at[d - 1],
            device_id={"tm": t - d},
            device_id_type=MESH,
        )

    def landing():
        if direct:
            return out_rows.at[0, 0, pl.ds(pl.multiple_of(u * cap, cap), cap)]
        return rows_recv.at[u]

    def rows_copy(k):
        v = lax.rem(u + k, n_sec)
        return pltpu.make_async_remote_copy(
            src_ref=rows_send.at[v],
            dst_ref=landing(),
            send_sem=rows_ss.at[k - 1],
            recv_sem=rows_rs.at[k - 1],
            device_id={"user": v},
            device_id_type=MESH,
        )

    def users_copy(k):
        v = lax.rem(u + k, n_sec)
        return pltpu.make_async_remote_copy(
            src_ref=users_send.at[v],
            dst_ref=users_recv.at[u],
            send_sem=users_ss.at[k - 1],
            recv_sem=users_rs.at[k - 1],
            device_id={"user": v},
            device_id_type=MESH,
        )

    c_one = math.sqrt(2.0 / math.pi)
    c_three = c_one * 0.044715

    def activated(i):
        cols = slice(i * step, (i + 1) * step)
        x = jnp.dot(ev_v[...], w1_v[:, cols], preferred_element_type=F32)
        x = x + b1_v[:, cols]
        twice = x + x * jnp.tanh(x * (c_one + c_three * (x * x)))
        return twice.astype(BF16)

    def second_product(i, active, rows):
        cols = slice(i * step, (i + 1) * step)
        pooled = jnp.dot(assign[rows], active, preferred_element_type=F32)
        return jnp.dot(pooled.astype(BF16), w2_v[cols, :], preferred_element_type=F32)

    for copy in small:
        copy.wait()
    w1_load[0].wait()
    ev_load.wait()
    active = activated(0)

    ids = ids_v[...]
    local = ids - (t - reach) * sess
    lane = iota((1, ev_rows), 1)
    local = jnp.where(lane < count_v[...], local, -1)
    belongs = jnp.where(local == iota((held, ev_rows), 0), 1.0, 0.0)
    assign = belongs.astype(BF16)

    for copy in w1_load[1:] + w2_load:
        copy.wait()
    far = (reach + 1) // 2 * sess
    total = second_product(0, active, slice(0, held))
    for i in range(1, parts - 1):
        total = total + second_product(i, activated(i), slice(0, held))
    active = activated(parts - 1)
    first_half = total[:far] + second_product(parts - 1, active, slice(0, far))
    sums_send[: far // sess] = first_half.reshape(-1, sess, width).astype(BF16)

    pl.semaphore_wait(barrier, jnp.minimum(t, reach) + n_sec - 1)

    def send_sums(d):
        @pl.when(t >= d)
        def _():
            sums_copy(d).start()

    for d in range(reach, reach - far // sess, -1):
        send_sums(d)
    rest = total[far:] + second_product(parts - 1, active, slice(far, held))
    near = rest[: held - far - sess]
    sums_send[far // sess :] = near.reshape(-1, sess, width).astype(BF16)
    for d in range(reach - far // sess, 0, -1):
        send_sums(d)
    acc[...] = rest[held - far - sess :]

    totals = jnp.sum(belongs, axis=1, keepdims=True)
    diagonal = iota((sess, 128), 0) == iota((sess, 128), 1)
    for d in range(reach + 1):
        first = (reach - d) * sess
        as_row = jnp.where(diagonal, totals[first : first + sess], 0.0)
        cnt_send[d] = jnp.broadcast_to(
            jnp.sum(as_row, axis=0, keepdims=True), (8, 128)
        )
    for d in range(reach, 0, -1):

        @pl.when(t >= d)
        def _(d=d):
            cnt_copy(d).start()

    user_row = user_v[...]
    square = iota((sess, sess), 0), iota((sess, sess), 1)
    user_col = jnp.sum(
        jnp.where(square[0] == square[1], user_row, 0), axis=1, keepdims=True
    )
    sec_row = lax.rem(user_row, n_sec)
    sec_col = lax.rem(user_col, n_sec)
    same = jnp.where(sec_row == sec_col, 1, 0)
    rank_row = jnp.sum(
        jnp.where(square[0] < square[1], same, 0), axis=0, keepdims=True
    )
    rank_col = jnp.sum(
        jnp.where(square[1] < square[0], same, 0), axis=1, keepdims=True
    )
    place = jnp.where(
        sec_row * padded + rank_row == iota((n_sec * padded, sess), 0), 1.0, 0.0
    ).astype(BF16)
    at = iota((sess, slots), 1) == rank_col + u * cap
    for v in range(n_sec):
        named = jnp.where(at & (sec_col == v), user_col + 1, 0)
        users_send[v] = jnp.broadcast_to(
            jnp.sum(named, axis=0, keepdims=True), (8, slots)
        )
    for k in range(1, n_sec):
        users_copy(k).start()
    users_recv[u] = users_send[u]

    for d in range(1, reach + 1):

        @pl.when(t + d < n_tm)
        def _(d=d):
            cnt_copy(d).wait_recv()
            cnt_send[0] += cnt_recv[d - 1]

    count = jnp.sum(
        jnp.where(diagonal, cnt_send[0][:1], 0.0), axis=1, keepdims=True
    )
    share = 0.5 / jnp.maximum(count, 1.0)
    embedded = jnp.log(1.0 + count) * embed_v[...]
    for k in range(1, n_sec):
        users_copy(k).wait_recv()
    out_users[0] = jnp.sum(users_recv[...], axis=0)[:1] - 1

    for d in range(1, reach + 1):

        @pl.when(t + d < n_tm)
        def _(d=d):
            sums_copy(d).wait_recv()
            acc[...] += sums_recv[d - 1].astype(F32)

    mixed = acc[...] * share + embedded
    mean = jnp.mean(mixed * mixed, axis=1, keepdims=True)
    rows = (mixed * lax.rsqrt(mean + 1e-06) * gain_v[...]).astype(BF16)
    outgoing = jnp.dot(place, rows, preferred_element_type=F32).astype(BF16)
    rows_send[...] = outgoing.reshape(n_sec, padded, width)
    for k in range(1, n_sec):
        rows_copy(k).start()
    landing()[...] = rows_send[u]

    for d in range(1, reach + 1):

        @pl.when(t >= d)
        def _(d=d):
            cnt_copy(d).wait_send()
            sums_copy(d).wait_send()

    for k in range(1, n_sec):
        users_copy(k).wait_send()
        rows_copy(k).wait_send()
    for k in range(1, n_sec):
        rows_copy(k).wait_recv()
    if not direct:
        whole = rows_recv[...].astype(F32)[:, :cap]
        out_rows[0, 0] = whole.reshape(slots, width).astype(BF16)


def on_device(
    n_tm,
    n_sec,
    events,
    w_first,
    b_first,
    w_second,
    count_embed,
    norm_gain,
    event_session,
    event_count,
    session_user,
):
    _, ev_rows, width = events.shape
    hidden = w_first.shape[1]
    sess = session_user.shape[1]
    reach = n_tm // 2
    cap = max(2, 2 * sess // n_sec)
    padded = -(-cap // 16) * 16
    slots = n_sec * cap
    parts = hidden // min(256, hidden)
    dma = pltpu.SemaphoreType.DMA
    vmem = pl.BlockSpec(memory_space=pltpu.VMEM)
    hbm = pl.BlockSpec(memory_space=pl.ANY)
    return pl.pallas_call(
        functools.partial(kernel, n_tm, n_sec, reach, cap),
        out_shape=(
            pltpu.VMEM((1, 1, slots, width), BF16),
            pltpu.VMEM((1, 1, slots), I32),
        ),
        in_specs=[hbm] * 9,
        out_specs=(vmem, vmem),
        scratch_shapes=[
            pltpu.VMEM((ev_rows, width), BF16),
            pltpu.VMEM((width, hidden), BF16),
            pltpu.VMEM((hidden, width), BF16),
            pltpu.VMEM((1, hidden), F32),
            pltpu.VMEM((1, width), F32),
            pltpu.VMEM((1, width), F32),
            pltpu.VMEM((1, ev_rows), I32),
            pltpu.VMEM((1, 1), I32),
            pltpu.VMEM((1, sess), I32),
            pltpu.VMEM((sess, width), F32),
            pltpu.VMEM((reach + 1, 8, 128), F32),
            pltpu.VMEM((reach, 8, 128), F32),
            pltpu.VMEM((reach, sess, width), BF16),
            pltpu.VMEM((reach, sess, width), BF16),
            pltpu.VMEM((n_sec, padded, width), BF16),
            pltpu.VMEM((n_sec, padded, width), BF16),
            pltpu.VMEM((n_sec, 8, slots), I32),
            pltpu.VMEM((n_sec, 8, slots), I32),
            dma((6,)),
            dma,
            dma((parts,)),
            dma((parts,)),
            dma((reach,)),
            dma((reach,)),
            dma((reach,)),
            dma((reach,)),
            dma((n_sec - 1,)),
            dma((n_sec - 1,)),
            dma((n_sec - 1,)),
            dma((n_sec - 1,)),
        ],
        compiler_params=pltpu.CompilerParams(
            collective_id=0, has_side_effects=True, vmem_limit_bytes=VMEM_BYTES
        ),
        name="pool_and_route",
    )(
        *(
            operand
            if operand.size == 1
            else pltpu.with_memory_space_constraint(operand, pltpu.HBM)
            for operand in (
                events,
                w_first,
                w_second,
                b_first.reshape(1, hidden),
                count_embed.reshape(1, width),
                norm_gain.reshape(1, width),
                event_session,
                event_count,
                session_user,
            )
        )
    )


def solution(mesh):
    in_specs = (
        P("user", "tm", None),
        P(),
        P(),
        P(),
        P(),
        P(),
        P("user", "tm"),
        P("user", "tm"),
        P("user", "tm"),
    )
    out_specs = (P("tm", "user", None, None), P("tm", "user", None))
    return jax.shard_map(
        functools.partial(on_device, mesh.shape["tm"], mesh.shape["user"]),
        mesh=mesh,
        in_specs=in_specs,
        out_specs=out_specs,
        check_vma=False,
    )
```

```python
import functools
import math

import jax
import jax.numpy as jnp
from jax import lax
from jax.experimental import pallas as pl
from jax.experimental.pallas import tpu as pltpu
from jax.sharding import PartitionSpec as P

MESH = pl.DeviceIdType.MESH
BF16 = jnp.bfloat16
F32 = jnp.float32
I32 = jnp.int32
VMEM_BYTES = 48 << 20


def iota(shape, axis):
    return lax.broadcasted_iota(I32, shape, axis)


def kernel(
    n_tm,
    n_sec,
    reach,
    cap,
    events,
    w_first,
    w_second,
    b_first,
    count_embed,
    norm_gain,
    event_session,
    event_count,
    session_user,
    out_rows,
    out_users,
    ev_v,
    w1_v,
    w2_v,
    b1_v,
    embed_v,
    gain_v,
    ids_v,
    count_v,
    user_v,
    acc,
    cnt_send,
    cnt_recv,
    sums_send,
    sums_recv,
    rows_send,
    rows_recv,
    users_send,
    users_recv,
    small_sem,
    ev_sem,
    w1_sem,
    w2_sem,
    sums_ss,
    sums_rs,
    cnt_ss,
    cnt_rs,
    rows_ss,
    rows_rs,
    users_ss,
    users_rs,
):
    t = lax.axis_index("tm")
    u = lax.axis_index("user")
    ev_rows, width = ev_v.shape
    hidden = w1_v.shape[1]
    sess = user_v.shape[1]
    held = (reach + 1) * sess
    step = min(256, hidden)
    parts = hidden // step

    def load(src, dst, sem):
        copy = pltpu.make_async_copy(src, dst, sem)
        copy.start()
        return copy

    small = [
        load(src, dst, small_sem.at[i])
        for i, (src, dst) in enumerate(
            (
                (event_session, ids_v),
                (event_count, count_v),
                (session_user, user_v),
                (b_first, b1_v),
                (count_embed, embed_v),
                (norm_gain, gain_v),
            )
        )
    ]
    w1_load, w2_load = [], []
    for i in range(parts):
        cols = pl.ds(i * step, step)
        w1_load.append(load(w_first.at[:, cols], w1_v.at[:, cols], w1_sem.at[i]))
        if i == 0:
            ev_load = load(events.at[0], ev_v, ev_sem)
    for i in range(parts):
        cols = pl.ds(i * step, step)
        w2_load.append(load(w_second.at[cols], w2_v.at[cols], w2_sem.at[i]))

    barrier = pltpu.get_barrier_semaphore()

    def greet(device):
        pl.semaphore_signal(barrier, inc=1, device_id=device, device_id_type=MESH)

    for d in range(1, reach + 1):

        @pl.when(t + d < n_tm)
        def _(d=d):
            greet({"tm": t + d})

    for k in range(1, n_sec):
        greet({"user": lax.rem(u + k, n_sec)})

    def sums_copy(d):
        return pltpu.make_async_remote_copy(
            src_ref=sums_send.at[reach - d],
            dst_ref=sums_recv.at[d - 1],
            send_sem=sums_ss.at[d - 1],
            recv_sem=sums_rs.at[d - 1],
            device_id={"tm": t - d},
            device_id_type=MESH,
        )

    def cnt_copy(d):
        return pltpu.make_async_remote_copy(
            src_ref=cnt_send.at[d],
            dst_ref=cnt_recv.at[d - 1],
            send_sem=cnt_ss.at[d - 1],
            recv_sem=cnt_rs.at[d - 1],
            device_id={"tm": t - d},
            device_id_type=MESH,
        )

    def routed_copy(k, send, recv, ss, rs):
        v = lax.rem(u + k, n_sec)
        return pltpu.make_async_remote_copy(
            src_ref=send.at[v],
            dst_ref=recv.at[u],
            send_sem=ss.at[k - 1],
            recv_sem=rs.at[k - 1],
            device_id={"user": v},
            device_id_type=MESH,
        )

    def rows_copy(k):
        return routed_copy(k, rows_send, rows_recv, rows_ss, rows_rs)

    def users_copy(k):
        return routed_copy(k, users_send, users_recv, users_ss, users_rs)

    c_one = math.sqrt(2.0 / math.pi)
    c_three = c_one * 0.044715

    def activated(i):
        cols = slice(i * step, (i + 1) * step)
        tiles = []
        for first in range(0, ev_rows, 128):
            x = jnp.dot(
                ev_v[first : first + 128],
                w1_v[:, cols],
                preferred_element_type=F32,
            )
            x = x + b1_v[:, cols]
            twice = x + x * jnp.tanh(x * (c_one + c_three * (x * x)))
            tiles.append(twice.astype(BF16))
        return jnp.concatenate(tiles, axis=0)

    def second_product(i, active, rows):
        cols = slice(i * step, (i + 1) * step)
        pooled = jnp.dot(assign[rows], active, preferred_element_type=F32)
        return jnp.dot(pooled.astype(BF16), w2_v[cols, :], preferred_element_type=F32)

    for copy in small:
        copy.wait()
    w1_load[0].wait()
    ev_load.wait()
    active = activated(0)

    ids = ids_v[...]
    local = ids - (t - reach) * sess
    lane = iota((1, ev_rows), 1)
    local = jnp.where(lane < count_v[...], local, -1)
    belongs = jnp.where(local == iota((held, ev_rows), 0), 1.0, 0.0)
    assign = belongs.astype(BF16)

    for copy in w1_load[1:] + w2_load:
        copy.wait()
    far = (reach + 1) // 2 * sess
    total = second_product(0, active, slice(0, held))
    for i in range(1, parts - 1):
        total = total + second_product(i, activated(i), slice(0, held))
    active = activated(parts - 1)
    first_half = total[:far] + second_product(parts - 1, active, slice(0, far))
    sums_send[: far // sess] = first_half.reshape(-1, sess, width).astype(BF16)

    pl.semaphore_wait(barrier, jnp.minimum(t, reach) + n_sec - 1)

    def send_sums(d):
        @pl.when(t >= d)
        def _():
            sums_copy(d).start()

    for d in range(reach, reach - far // sess, -1):
        send_sums(d)
    rest = total[far:] + second_product(parts - 1, active, slice(far, held))
    near = rest[: held - far - sess]
    sums_send[far // sess :] = near.reshape(-1, sess, width).astype(BF16)
    for d in range(reach - far // sess, 0, -1):
        send_sums(d)
    acc[...] = rest[held - far - sess :]

    totals = jnp.sum(belongs, axis=1, keepdims=True)
    diagonal = iota((sess, 128), 0) == iota((sess, 128), 1)
    for d in range(reach + 1):
        first = (reach - d) * sess
        as_row = jnp.where(diagonal, totals[first : first + sess], 0.0)
        cnt_send[d] = jnp.broadcast_to(
            jnp.sum(as_row, axis=0, keepdims=True), (8, 128)
        )
    for d in range(reach, 0, -1):

        @pl.when(t >= d)
        def _(d=d):
            cnt_copy(d).start()

    user_row = user_v[...]
    square = iota((sess, sess), 0), iota((sess, sess), 1)
    user_col = jnp.sum(
        jnp.where(square[0] == square[1], user_row, 0), axis=1, keepdims=True
    )
    sec_row = lax.rem(user_row, n_sec)
    sec_col = lax.rem(user_col, n_sec)
    same = jnp.where(sec_row == sec_col, 1, 0)
    rank_row = jnp.sum(
        jnp.where(square[0] < square[1], same, 0), axis=0, keepdims=True
    )
    rank_col = jnp.sum(
        jnp.where(square[1] < square[0], same, 0), axis=1, keepdims=True
    )
    padded = rows_send.shape[1]
    place = jnp.where(
        sec_row * padded + rank_row == iota((n_sec * padded, sess), 0), 1.0, 0.0
    ).astype(BF16)
    slots = n_sec * cap
    at = iota((sess, slots), 1) == rank_col + u * cap
    for v in range(n_sec):
        named = jnp.where(at & (sec_col == v), user_col + 1, 0)
        users_send[v] = jnp.broadcast_to(
            jnp.sum(named, axis=0, keepdims=True), (8, slots)
        )
    for k in range(1, n_sec):
        users_copy(k).start()
    users_recv[u] = users_send[u]

    for d in range(1, reach + 1):

        @pl.when(t + d < n_tm)
        def _(d=d):
            cnt_copy(d).wait_recv()
            cnt_send[0] += cnt_recv[d - 1]

    count = jnp.sum(
        jnp.where(diagonal, cnt_send[0][:1], 0.0), axis=1, keepdims=True
    )
    share = 0.5 / jnp.maximum(count, 1.0)
    embedded = jnp.log(1.0 + count) * embed_v[...]
    for k in range(1, n_sec):
        users_copy(k).wait_recv()
    out_users[0] = jnp.sum(users_recv[...], axis=0)[:1] - 1

    for d in range(1, reach + 1):

        @pl.when(t + d < n_tm)
        def _(d=d):
            sums_copy(d).wait_recv()
            acc[...] += sums_recv[d - 1].astype(F32)

    mixed = acc[...] * share + embedded
    mean = jnp.mean(mixed * mixed, axis=1, keepdims=True)
    rows = (mixed * lax.rsqrt(mean + 1e-06) * gain_v[...]).astype(BF16)
    outgoing = jnp.dot(place, rows, preferred_element_type=F32).astype(BF16)
    rows_send[...] = outgoing.reshape(n_sec, padded, width)
    for k in range(1, n_sec):
        rows_copy(k).start()
    rows_recv[u] = rows_send[u]

    for d in range(1, reach + 1):

        @pl.when(t >= d)
        def _(d=d):
            cnt_copy(d).wait_send()
            sums_copy(d).wait_send()

    for k in range(1, n_sec):
        users_copy(k).wait_send()
        rows_copy(k).wait_send()
    for k in range(1, n_sec):
        rows_copy(k).wait_recv()
    if padded == cap:
        out_rows[0, 0] = rows_recv[...].reshape(slots, width)
    else:
        whole = rows_recv[...].astype(F32)[:, :cap]
        out_rows[0, 0] = whole.reshape(slots, width).astype(BF16)


def on_device(
    n_tm,
    n_sec,
    events,
    w_first,
    b_first,
    w_second,
    count_embed,
    norm_gain,
    event_session,
    event_count,
    session_user,
):
    _, ev_rows, width = events.shape
    hidden = w_first.shape[1]
    sess = session_user.shape[1]
    reach = n_tm // 2
    cap = max(2, 2 * sess // n_sec)
    padded = -(-cap // 16) * 16
    slots = n_sec * cap
    parts = hidden // min(256, hidden)
    dma = pltpu.SemaphoreType.DMA
    vmem = pl.BlockSpec(memory_space=pltpu.VMEM)
    hbm = pl.BlockSpec(memory_space=pl.ANY)
    return pl.pallas_call(
        functools.partial(kernel, n_tm, n_sec, reach, cap),
        out_shape=(
            pltpu.VMEM((1, 1, slots, width), BF16),
            pltpu.VMEM((1, 1, slots), I32),
        ),
        in_specs=[hbm] * 9,
        out_specs=(vmem, vmem),
        scratch_shapes=[
            pltpu.VMEM((ev_rows, width), BF16),
            pltpu.VMEM((width, hidden), BF16),
            pltpu.VMEM((hidden, width), BF16),
            pltpu.VMEM((1, hidden), F32),
            pltpu.VMEM((1, width), F32),
            pltpu.VMEM((1, width), F32),
            pltpu.VMEM((1, ev_rows), I32),
            pltpu.VMEM((1, 1), I32),
            pltpu.VMEM((1, sess), I32),
            pltpu.VMEM((sess, width), F32),
            pltpu.VMEM((reach + 1, 8, 128), F32),
            pltpu.VMEM((reach, 8, 128), F32),
            pltpu.VMEM((reach, sess, width), BF16),
            pltpu.VMEM((reach, sess, width), BF16),
            pltpu.VMEM((n_sec, padded, width), BF16),
            pltpu.VMEM((n_sec, padded, width), BF16),
            pltpu.VMEM((n_sec, 8, slots), I32),
            pltpu.VMEM((n_sec, 8, slots), I32),
            dma((6,)),
            dma,
            dma((parts,)),
            dma((parts,)),
            dma((reach,)),
            dma((reach,)),
            dma((reach,)),
            dma((reach,)),
            dma((n_sec - 1,)),
            dma((n_sec - 1,)),
            dma((n_sec - 1,)),
            dma((n_sec - 1,)),
        ],
        compiler_params=pltpu.CompilerParams(
            collective_id=0, has_side_effects=True, vmem_limit_bytes=VMEM_BYTES
        ),
        name="pool_and_route",
    )(
        *(
            operand
            if operand.size == 1
            else pltpu.with_memory_space_constraint(operand, pltpu.HBM)
            for operand in (
                events,
                w_first,
                w_second,
                b_first.reshape(1, hidden),
                count_embed.reshape(1, width),
                norm_gain.reshape(1, width),
                event_session,
                event_count,
                session_user,
            )
        )
    )


def solution(mesh):
    in_specs = (
        P("user", "tm", None),
        P(),
        P(),
        P(),
        P(),
        P(),
        P("user", "tm"),
        P("user", "tm"),
        P("user", "tm"),
    )
    out_specs = (P("tm", "user", None, None), P("tm", "user", None))
    return jax.shard_map(
        functools.partial(on_device, mesh.shape["tm"], mesh.shape["user"]),
        mesh=mesh,
        in_specs=in_specs,
        out_specs=out_specs,
        check_vma=False,
    )
```
